32 devices in a mesh: half: 2 (over y), rows: 16 (over z, x, core).
Axes of the slice: x: 2, y: 2, z: 4, core: 2. Of those that a mesh axis runs over, the one named last changes fastest.
Arguments:
- frames: bfloat16 [16384, 3000], P(('half', 'rows')), may hold values from -8 to 8
- labels: int32 [16384], P(('half', 'rows')), may hold values from 0 to 1, as said below
- counts: int32 [32], P(('half', 'rows')), may hold values from 256 to 512, as said below
- seeds: int32 [2, 512], P('half', 'rows'), may hold values from 0 to 511
Outputs:
- means: float32 [2, 512, 3000], P('half', 'rows')
- occupancy: float32 [2, 512], P('half', 'rows')
The draws below stay inside these ranges and needn't reach their ends.
Inputs may be any that keep to these rules, and one draw needn't show every extreme that they name: `labels`: on each device of half h, live frames carry child h except for at most 256 of them, which carry 1 - h; exactly 256 do on some device. Frames that are not live carry h. `counts`: 512 on some device.
All inputs are finite; a program needn't handle non-finite values.
Results may differ from the reference program's by a relative error of at most 0.0014.
Values may be sent and summed in bfloat16 or wider, within the bound.
A program may use at most 128 MiB of HBM per device.

```python
import math
import jax
import jax.numpy as jnp
from jax import lax

F = 3000
K = 512
ROWS_DEV = 512
CAP = 256
N = 16384
N_HALF = 2
N_ROWS = 16


def draw_frames(key, part):
    values = jnp.clip(jax.random.normal(key, (N, F)), -6.0, 6.0)
    return values.astype(jnp.float32).astype(jnp.bfloat16)


def layout_helper(key):
    devices = N_HALF * N_ROWS
    base = jax.random.fold_in(key, 7)
    count_key, mover_key, first_key, second_key, perm_key = jax.random.split(base, 5)
    counts = jax.random.randint(count_key, (devices,), CAP, ROWS_DEV + 1)
    counts = counts.at[jax.random.randint(first_key, (), 0, devices)].set(ROWS_DEV)
    movers = jax.random.randint(mover_key, (devices,), max(CAP // 4, 1), CAP + 1)
    movers = movers.at[jax.random.randint(second_key, (), 0, devices)].set(CAP)
    perms = jax.vmap(lambda k: jax.random.permutation(k, ROWS_DEV))(jax.random.split(perm_key, devices))
    spots = jnp.arange(ROWS_DEV, dtype=jnp.int32)
    scores = jnp.where(spots[None, :] < counts[:, None], perms, ROWS_DEV + spots[None, :]).astype(jnp.int32)
    ranks = jnp.argsort(jnp.argsort(scores, axis=1, stable=True), axis=1, stable=True)
    moving = ranks < movers[:, None]
    side = (jnp.arange(devices, dtype=jnp.int32) // N_ROWS)[:, None]
    labels = jnp.where(moving, 1 - side, side).astype(jnp.int32)
    return (labels.reshape(-1), counts.astype(jnp.int32))


def draw_labels(key, part):
    return layout_helper(key)[0]


def draw_counts(key, part):
    return layout_helper(key)[1]


def set_ends(result, key, least, high):
    extent = result.shape
    spot = [jax.random.randint(jax.random.fold_in(key, axis), (), 0, extent[axis]) for axis in range(len(extent))]
    result = result.at[tuple(spot)].set(least)
    longest = extent.index(max(extent))
    spot[longest] = (spot[longest] + 1) % extent[longest]
    return result.at[tuple(spot)].set(high)


def setup_inputs(seed: int = 0) -> dict:
    arg_keys = jax.random.split(jax.random.key(seed), 5)
    return {
        "frames": draw_frames(jax.random.fold_in(arg_keys[4], 71), 0),
        "labels": draw_labels(jax.random.fold_in(arg_keys[4], 71), 0),
        "counts": draw_counts(jax.random.fold_in(arg_keys[4], 71), 0),
        "seeds": set_ends(jax.random.randint(arg_keys[3], (2, K), 0, ROWS_DEV), jax.random.fold_in(arg_keys[3], 1), 0, ROWS_DEV - 1).astype(jnp.int32),
    }


def score_rows(rows_in, table):
    cross = lax.dot_general(rows_in, table, (((1,), (1,)), ((), ())), preferred_element_type=jnp.float32)
    wide = table.astype(jnp.float32)
    return (cross - 0.5 * lax.optimization_barrier(jnp.sum(wide * wide, axis=1))[None, :]) / math.sqrt(F)

def soft_weights(logits, valid):
    top = lax.optimization_barrier(jnp.max(logits, axis=1, keepdims=True))
    expo = jnp.exp(logits - top)
    total = lax.optimization_barrier(jnp.sum(expo, axis=1, keepdims=True))
    return (expo / total * valid[:, None]).astype(jnp.bfloat16)

def weighted(weights, rows_in):
    return lax.dot_general(weights, rows_in, (((0,), (0,)), ((), ())), preferred_element_type=jnp.float32)

def reference(frames, labels, counts, seeds):
    devices = N_HALF * N_ROWS
    shard_k = K // N_ROWS
    owners = jnp.arange(2 * K, dtype=jnp.int32) // shard_k
    where_from = (owners * ROWS_DEV + seeds.reshape(-1)).astype(jnp.int32)
    table = frames[where_from].reshape(2, K, F)
    blocks = frames.reshape(devices, ROWS_DEV, F)
    label_blocks = labels.reshape(devices, ROWS_DEV)
    spots = jnp.arange(ROWS_DEV, dtype=jnp.int32)

    def visit(carry, item):
        sums, mass = carry
        block, lab, count, dev = item
        side = dev // N_ROWS
        live = spots < count
        foreign = live & (lab != side)
        native = (live & (lab == side)).astype(jnp.float32)
        order = jnp.argsort(jnp.where(foreign, 0, 1).astype(jnp.int32), stable=True)
        picked = order[:CAP]
        moved = block[picked]
        flag = foreign[picked].astype(jnp.float32)
        own_w = soft_weights(score_rows(block, table[side]), native)
        far_w = soft_weights(score_rows(moved, table[1 - side]), flag)
        sums = sums.at[side].add(weighted(own_w, block))
        sums = sums.at[1 - side].add(weighted(far_w, moved))
        mass = mass.at[side].add(lax.optimization_barrier(jnp.sum(own_w.astype(jnp.float32), axis=0)))
        mass = mass.at[1 - side].add(lax.optimization_barrier(jnp.sum(far_w.astype(jnp.float32), axis=0)))
        return ((sums, mass), None)
    init = (jnp.zeros((2, K, F), jnp.float32), jnp.zeros((2, K), jnp.float32))
    (sums, mass), _ = lax.scan(visit, init, (blocks, label_blocks, counts, jnp.arange(devices, dtype=jnp.int32)))
    means = sums / (mass + 1.0)[:, :, None]
    occupancy = mass * (2.0 * K / N)
    return (means, occupancy)
```

```python
import functools
import math

import jax
import jax.numpy as jnp
from jax import lax
from jax.experimental import pallas as pl
from jax.experimental.pallas import tpu as pltpu
from jax.sharding import PartitionSpec as P


def from_partner(value, axis, stride):
    mask = 2**stride
    pairs = [(source, source ^ mask) for source in range(lax.axis_size(axis))]
    return lax.ppermute(value, axis, pairs)


def score_piece(rows_in, piece):
    cross = lax.dot_general(
        rows_in, piece, (((1,), (1,)), ((), ())), preferred_element_type=jnp.float32
    )
    wide = piece.astype(jnp.float32)
    return (cross - 0.5 * jnp.sum(wide * wide, axis=1)[None, :]) / math.sqrt(rows_in.shape[1])


def soft_weights(logits, valid):
    top = jnp.max(logits, axis=1, keepdims=True)
    expo = jnp.exp(logits - top)
    total = jnp.sum(expo, axis=1, keepdims=True)
    return (expo / total * valid[:, None]).astype(jnp.bfloat16)


def weighted(weights, rows_in):
    return lax.dot_general(
        weights, rows_in, (((0,), (0,)), ((), ())), preferred_element_type=jnp.float32
    )


def column_mass(weights):
    return jnp.sum(weights.astype(jnp.float32), axis=0)


def shards(frames, labels, counts, seeds):
    rows_dev = frames.shape[0]
    cap = rows_dev // 2
    side = lax.axis_index("half")
    spots = jnp.arange(rows_dev, dtype=jnp.int32)
    live = spots < counts[0]
    foreign = live & (labels != side)
    native = (live & (labels == side)).astype(jnp.float32)
    order = jnp.argsort(jnp.where(foreign, 0, 1).astype(jnp.int32), stable=True)
    picked = order[:cap]
    moved = frames[picked]
    flag = foreign[picked].astype(jnp.float32)
    mine = frames[seeds[0]]
    got_rows, got_flag = from_partner((moved, flag.astype(jnp.bfloat16)), "half", 0)
    pool = jnp.concatenate([frames, got_rows], axis=0)
    valid = jnp.concatenate([native, got_flag.astype(jnp.float32)])
    logits = score_piece(pool, lax.all_gather(mine, "rows", axis=0, tiled=True))
    weights = soft_weights(logits, valid)
    sums, mass = (
        lax.psum_scatter(weighted(weights, pool), "rows", scatter_dimension=0, tiled=True),
        lax.psum_scatter(column_mass(weights), "rows", scatter_dimension=0, tiled=True),
    )
    whole_k = mass.shape[0] * lax.axis_size("rows")
    total_slots = rows_dev * lax.axis_size("half") * lax.axis_size("rows")
    means = sums / (mass + 1.0)[:, None]
    occupancy = mass * (2.0 * whole_k / total_slots)
    return (means[None], occupancy[None])


MESH = pl.DeviceIdType.MESH
WIRE = jnp.bfloat16
STEP = 512
CHUNK = 256
EARLY = 0
PART = 128
LAG = 4
NT = (((1,), (1,)), ((), ()))
NN = (((1,), (0,)), ((), ()))


def round_up(value, unit):
    return -(-value // unit) * unit


def dot(a, b, how):
    return lax.dot_general(a, b, how, preferred_element_type=jnp.float32)


def column_weights(cross, norm, width, valid):
    logits = (cross - 0.5 * norm) / math.sqrt(width)
    top = jnp.max(logits, axis=0, keepdims=True)
    expo = jnp.exp(logits - top)
    total = jnp.sum(expo, axis=0, keepdims=True)
    return (expo / total * valid).astype(jnp.bfloat16)


def level(
    outer, width, scale,
    x_ref, tail_ref, labels_hbm, counts_ref, seeds_hbm,
    means_ref, occupancy_ref,
    labels_ref, seeds_ref, xf, table, gone, came, squares, cross, near, weights,
    keep, csend, crecv, keepx, xsend, xrecv, zsend, zrecv,
    small_load, x_load, y_out, y_in, u_out, d_out, t_out, t_in, c_out, c_in, x_out, x_in, z_out, z_in,
):
    slots = xf.shape[2]
    shard = seeds_ref.shape[1]
    steps = xf.shape[0]
    parts = gone.shape[0]
    sent = y_rows(width)
    whole = steps - 1
    rest = width - whole * STEP
    half_k = keep.shape[1]
    quarter_k = keepx.shape[1]
    side = lax.axis_index("half")
    row = lax.axis_index("rows")
    twin = row + 1 - 2 * (row % 2)
    across = row + 2 - 4 * ((row // 2) % 2)
    along = [
        ((row // 4 + d) % outer) * 4 + row % 4 for d in range(1, outer)
    ]

    barrier = pltpu.get_barrier_semaphore()
    pl.semaphore_signal(barrier, inc=1, device_id=(1 - side, row), device_id_type=MESH)
    for peer in [twin, across] + along:
        pl.semaphore_signal(barrier, inc=1, device_id=(side, peer), device_id_type=MESH)

    def load(c):
        at = pl.ds(pl.multiple_of(c * STEP, STEP), STEP)
        return pltpu.make_async_copy(x_ref.at[at], xf.at[c], x_load.at[c])

    def remote(src, dst, out_sem, in_sem, where):
        return pltpu.make_async_remote_copy(
            src_ref=src, dst_ref=dst, send_sem=out_sem, recv_sem=in_sem,
            device_id=where, device_id_type=MESH,
        )

    labels_load = pltpu.make_async_copy(labels_hbm, labels_ref, small_load.at[0])
    seeds_load = pltpu.make_async_copy(seeds_hbm, seeds_ref, small_load.at[1])
    labels_load.start()
    seeds_load.start()

    @pl.loop(0, whole)
    def _(c):
        load(c).start()

    labels_load.wait()
    seeds_load.wait()
    labels = labels_ref[...]
    spots = lax.broadcasted_iota(jnp.int32, (1, slots), 1)
    live = spots < counts_ref[0]
    native = (live & (labels == side)).astype(jnp.float32)
    foreign = jnp.where(live & (labels != side), 1.0, 0.0)
    upper = (
        lax.broadcasted_iota(jnp.int32, (slots, slots), 0)
        <= lax.broadcasted_iota(jnp.int32, (slots, slots), 1)
    ).astype(jnp.float32).astype(jnp.bfloat16)
    rank = dot(jnp.broadcast_to(foreign, (16, slots)).astype(jnp.bfloat16), upper, NN)[:1]
    place = jnp.where(foreign > 0, rank - 1.0, -1.0).astype(jnp.int32)

    xf[whole, pl.ds(0, rest), :] = tail_ref[pl.ds(0, rest), :]
    fill = lax.broadcasted_iota(jnp.int32, (STEP - rest, slots), 0) == 0
    xf[whole, pl.ds(rest, STEP - rest), :] = fill.astype(jnp.float32).astype(jnp.bfloat16)

    def pick(part):
        lane = lax.broadcasted_iota(jnp.int32, (PART, slots), 0) + part * PART
        return (lane == place).astype(jnp.float32).astype(jnp.bfloat16)

    def y_copy(part, c, rows=STEP):
        at = pl.ds(c * STEP, rows)
        return remote(
            gone.at[part, at], came.at[part, at],
            y_out.at[part, c], y_in.at[part, c], (1 - side, row),
        )

    last_rows = sent - whole * STEP

    def each_y(part, act):
        @pl.loop(0, whole)
        def _(c):
            act(y_copy(part, c))

        act(y_copy(part, whole, last_rows))

    first = pick(0)

    def leave(c):
        at = pl.ds(pl.multiple_of(c * STEP, STEP), STEP)
        load(c).wait()
        gone[0, at, :] = dot(xf[c], first, NT).astype(jnp.bfloat16)

    for c in range(EARLY):
        leave(c)
    pl.semaphore_wait(barrier, outer + 2)
    for c in range(EARLY):
        y_copy(0, c).start()

    @pl.loop(EARLY, whole)
    def _(c):
        leave(c)
        y_copy(0, c).start()

    gone[0, pl.ds(whole * STEP, STEP), :] = dot(xf[whole], first, NT).astype(jnp.bfloat16)
    y_copy(0, whole, last_rows).start()

    seeds = jnp.broadcast_to(seeds_ref[...], (shard, shard))
    diagonal = lax.broadcasted_iota(jnp.int32, (shard, shard), 0) == lax.broadcasted_iota(
        jnp.int32, (shard, shard), 1
    )
    seed = jnp.sum(jnp.where(diagonal, seeds, 0), axis=1, keepdims=True)
    chosen = (
        lax.broadcasted_iota(jnp.int32, (shard, slots), 1) == seed
    ).astype(jnp.float32).astype(jnp.bfloat16)

    @pl.loop(0, steps)
    def _(c):
        at = pl.ds(pl.multiple_of(c * STEP, STEP), STEP)
        lane = lax.broadcasted_iota(jnp.int32, (shard, STEP), 1) + c * STEP
        mine = dot(chosen, xf[c], NT)
        table[pl.ds(0, shard), at] = jnp.where(lane < width, mine, 0.0).astype(jnp.bfloat16)

    def t_copy(index, source, target, where):
        return remote(
            table.at[pl.ds(source * shard, shard)], table.at[pl.ds(target * shard, shard)],
            t_out.at[index], t_in.at[target], (side, where),
        )

    def up_copy(k):
        where = lax.rem(row + 4, outer * 4)
        return remote(
            table.at[pl.ds((outer - k) % outer * shard, shard)],
            table.at[pl.ds((outer - k - 1) * shard, shard)],
            u_out.at[k], t_in.at[outer - k - 1], (side, where),
        )

    def down_copy(k):
        where = lax.rem(row + (outer - 1) * 4, outer * 4)
        return remote(
            table.at[pl.ds(k * shard, shard)], table.at[pl.ds((k + 1) * shard, shard)],
            d_out.at[k], t_in.at[k + 1], (side, where),
        )

    x_gather = [t_copy(s, s, outer + s, across) for s in range(outer)]
    c_gather = [t_copy(outer + s, s, 2 * outer + s, twin) for s in range(2 * outer)]
    depth = row // 4

    @pl.when(depth > 0)
    def _():
        down_copy(0).start()

    @pl.when(depth < outer - 1)
    def _():
        up_copy(0).start()

    x_gather[0].start()
    c_gather[0].start()

    for part in range(1, parts):
        later = pick(part)

        @pl.loop(0, steps)
        def _(c):
            at = pl.ds(pl.multiple_of(c * STEP, STEP), STEP)
            gone[part, at, :] = dot(xf[c], later, NT).astype(jnp.bfloat16)

        each_y(part, lambda copy: copy.start())
    if steps * STEP > sent:
        for part in range(parts):
            came[part, pl.ds(sent, steps * STEP - sent), :] = jnp.zeros(
                (steps * STEP - sent, PART), jnp.bfloat16
            )

    def arrived(slot):
        return t_copy(0, 0, slot, twin).wait_recv()

    def from_above(k):
        arrived(k)

        @pl.when(depth > 0)
        def _():
            down_copy(k).start()

        x_gather[k].start()
        c_gather[k].start()

    def from_below(k):
        arrived(outer - k)

        @pl.when(depth < outer - 1)
        def _():
            up_copy(k).start()

        x_gather[outer - k].start()
        c_gather[outer - k].start()

    def crossed(s):
        x_gather[s].wait_recv()
        c_gather[outer + s].start()

    def both(k, above, below):
        @pl.when(depth + k <= outer - 1)
        def _():
            above(k)

        @pl.when(depth >= k)
        def _():
            below(k)

    for k in range(1, outer):
        both(k, from_above, from_below)
        if k == 1:
            crossed(0)
        else:
            both(k - 1, crossed, lambda back: crossed(outer - back))
    squares[...] = jnp.zeros_like(squares)
    near[...] = jnp.zeros_like(near)

    def score(group):
        rows_at = pl.ds(group * quarter_k, quarter_k)

        @pl.loop(0, steps)
        def _(c):
            at = pl.ds(pl.multiple_of(c * STEP, STEP), STEP)
            block = table[rows_at, at]
            near[rows_at, :] += dot(block, xf[c], NN)
            wide = block.astype(jnp.float32)
            wide = wide * wide
            total = wide[:, :PART]
            for lane in range(PART, STEP, PART):
                total += wide[:, lane : lane + PART]
            squares[rows_at, :] += total

    score(0)
    for s in range(outer):
        c_gather[s].wait_recv()
    score(2)
    both(outer - 1, crossed, lambda back: crossed(outer - back))
    score(1)
    for s in range(outer, 2 * outer):
        c_gather[s].wait_recv()
    score(3)

    norm = jnp.sum(squares[...], axis=1, keepdims=True)
    weights[:, pl.ds(0, slots)] = column_weights(near[...], norm, width, native)

    for part in range(parts):
        cross[...] = jnp.zeros_like(cross)

        @pl.loop(0, steps)
        def _(c):
            @pl.when(c < whole)
            def _():
                y_copy(part, c).wait_recv()

            @pl.when(c == whole)
            def _():
                y_copy(part, whole, last_rows).wait_recv()

            at = pl.ds(pl.multiple_of(c * STEP, STEP), STEP)
            cross[...] += dot(table[:, at], came[part, at, :], NN)

        flag = came[part, pl.ds(width // 16 * 16, 16), :].astype(jnp.float32)
        flag = flag[width % 16 : width % 16 + 1]
        weights[:, pl.ds(slots + part * PART, PART)] = column_weights(
            cross[...], norm, width, flag
        )

    last = width % CHUNK
    chunks = width // CHUNK + 1

    def column(c):
        return pl.multiple_of(lax.rem(c + chunks - 1, chunks) * CHUNK, CHUNK)

    def narrow(c, ref, sums):
        ref[...] = sums.astype(WIRE)

        @pl.when(c == 0)
        def _():
            low = last // PART * PART
            tile = sums[:, low : low + PART]
            lost = pltpu.roll(tile - tile.astype(WIRE).astype(jnp.float32), 1, 1)
            lane = lax.broadcasted_iota(jnp.int32, tile.shape, 1)
            tile = jnp.where(lane == last - low + 1, tile + lost, tile)
            ref[:, low : low + PART] = tile.astype(WIRE)

    def c_copy(c):
        return remote(csend.at[c], crecv.at[c], c_out.at[c], c_in.at[c], (side, twin))

    def x_copy(c):
        return remote(xsend.at[c], xrecv.at[c], x_out.at[c], x_in.at[c], (side, across))

    def z_copy(c, d):
        return remote(
            zsend.at[c, d - 1], zrecv.at[c, d - 1],
            z_out.at[c, d - 1], z_in.at[c, d - 1], (side, along[d - 1]),
        )

    def add_up(c):
        place = column(c)
        at = pl.ds(place, CHUNK)
        within = pl.ds(pl.multiple_of(place % STEP, CHUNK), CHUNK)
        block = jnp.concatenate(
            [xf[place // STEP, within]] + [came[part, at, :] for part in range(parts)], axis=1
        )
        sums = dot(weights[...], block, NT)
        csend[c] = sums[half_k:]
        c_copy(c).start()
        keep[c] = sums[:half_k]

    def to_across(c):
        c_copy(c).wait_recv()
        sums = keep[c] + crecv[c]
        narrow(c, xsend.at[c], sums[quarter_k:])
        x_copy(c).start()
        keepx[c] = sums[:quarter_k]

    def to_along(c):
        x_copy(c).wait_recv()
        sums = keepx[c] + xrecv[c].astype(jnp.float32)
        for d in range(1, outer):
            narrow(c, zsend.at[c, d - 1], sums[d * shard : (d + 1) * shard])
        for d in range(1, outer):
            z_copy(c, d).start()
        keepx[c, pl.ds(0, shard), :] = sums[:shard]

    @pl.loop(0, chunks + LAG)
    def _(c):
        @pl.when(c < chunks)
        def _():
            add_up(c)

        @pl.when((c > 0) & (c <= chunks))
        def _():
            to_across(c - 1)

        @pl.when(c >= LAG)
        def _():
            to_along(c - LAG)

    def total(c):
        sums = keepx[c, pl.ds(0, shard), :]
        for d in range(1, outer):
            z_copy(c, d).wait_recv()
            sums += zrecv[c, d - 1].astype(jnp.float32)
        return sums

    sums = total(0)
    mass = sums[:, last : last + 1] + sums[:, last + 1 : last + 2]
    means_ref[:, pl.ds(width - last, last)] = sums[:, :last] / (mass + 1.0)
    turned = jnp.sum(jnp.where(diagonal, mass, 0.0), axis=0, keepdims=True)
    occupancy_ref[...] = turned * scale

    @pl.loop(1, chunks)
    def _(c):
        means_ref[:, pl.ds(column(c), CHUNK)] = total(c) / (mass + 1.0)

    for copy in x_gather + c_gather:
        copy.wait_send()
    for k in range(outer - 1):
        @pl.when((depth > 0) & (depth + k <= outer - 1))
        def _():
            down_copy(k).wait_send()

        @pl.when((depth < outer - 1) & (depth >= k))
        def _():
            up_copy(k).wait_send()

    for part in range(parts):
        each_y(part, lambda copy: copy.wait_send())

    @pl.loop(0, chunks)
    def _(c):
        c_copy(c).wait_send()
        x_copy(c).wait_send()
        for d in range(1, outer):
            z_copy(c, d).wait_send()


def y_rows(width):
    return round_up(width + 1, 16)


def fused(frames, labels, counts, seeds):
    slots, width = frames.shape
    shard = seeds.shape[1]
    n_rows = lax.axis_size("rows")
    outer = n_rows // 4
    whole_k = shard * n_rows
    parts = slots // 2 // PART
    padded = round_up(width + 1, STEP)
    steps = padded // STEP
    chunks = width // CHUNK + 1
    total_slots = slots * lax.axis_size("half") * n_rows
    scale = 2.0 * whole_k / total_slots
    dma = pltpu.SemaphoreType.DMA
    bf16, f32 = jnp.bfloat16, jnp.float32
    flops = 4 * (slots + slots // 2) * whole_k * width
    vmem = pl.BlockSpec(memory_space=pltpu.VMEM)
    hbm = pl.BlockSpec(memory_space=pltpu.HBM)
    means, occupancy = pl.pallas_call(
        functools.partial(level, outer, width, scale),
        out_shape=(
            jax.ShapeDtypeStruct((shard, width), f32),
            jax.ShapeDtypeStruct((1, shard), f32),
        ),
        grid=(1,),
        in_specs=[
            hbm,
            pl.BlockSpec((STEP, slots), lambda i: (steps - 1, 0)),
            hbm, pl.BlockSpec(memory_space=pltpu.SMEM), hbm,
        ],
        out_specs=(vmem, vmem),
        scratch_shapes=[
            pltpu.VMEM((1, slots), jnp.int32),
            pltpu.VMEM((1, shard), jnp.int32),
            pltpu.VMEM((steps, STEP, slots), bf16),
            pltpu.VMEM((whole_k, padded), bf16),
            pltpu.VMEM((parts, padded, PART), bf16),
            pltpu.VMEM((parts, padded, PART), bf16),
            pltpu.VMEM((whole_k, PART), f32),
            pltpu.VMEM((whole_k, PART), f32),
            pltpu.VMEM((whole_k, slots), f32),
            pltpu.VMEM((whole_k, slots + parts * PART), bf16),
            pltpu.VMEM((chunks, whole_k // 2, CHUNK), f32),
            pltpu.VMEM((chunks, whole_k // 2, CHUNK), f32),
            pltpu.VMEM((chunks, whole_k // 2, CHUNK), f32),
            pltpu.VMEM((chunks, whole_k // 4, CHUNK), f32),
            pltpu.VMEM((chunks, whole_k // 4, CHUNK), WIRE),
            pltpu.VMEM((chunks, whole_k // 4, CHUNK), WIRE),
            pltpu.VMEM((chunks, outer - 1, shard, CHUNK), WIRE),
            pltpu.VMEM((chunks, outer - 1, shard, CHUNK), WIRE),
            dma((2,)), dma((steps,)), dma((parts, steps)), dma((parts, steps)),
            dma((outer,)), dma((outer,)),
            dma((4 * outer,)), dma((4 * outer,)),
            dma((chunks,)), dma((chunks,)),
            dma((chunks,)), dma((chunks,)),
            dma((chunks, outer - 1)), dma((chunks, outer - 1)),
        ],
        compiler_params=pltpu.CompilerParams(
            collective_id=0, has_side_effects=True, vmem_limit_bytes=52 * 2**20
        ),
        cost_estimate=pl.CostEstimate(
            flops=flops, bytes_accessed=slots * width * 2, transcendentals=slots * whole_k
        ),
    )(
        frames.T, frames.T,
        pltpu.with_memory_space_constraint(labels[None], pltpu.HBM), counts,
        pltpu.with_memory_space_constraint(seeds, pltpu.HBM),
    )
    return (means[None], occupancy)


def fits(mesh, frames, seeds):
    sizes = dict(mesh.shape)
    n_half, n_rows = sizes["half"], sizes["rows"]
    slots = frames.shape[0] // (n_half * n_rows)
    shard = seeds.shape[1] // n_rows
    lone = frames.shape[1] % STEP > 0 and frames.shape[1] % PART < PART - 1
    return (
        n_half == 2 and n_rows % 4 == 0 and n_rows >= 8 and shard % 16 == 0 and shard > 0
        and slots % (2 * PART) == 0 and slots * n_half * n_rows == frames.shape[0]
        and slots <= 1024 and seeds.shape[1] <= 512 and frames.shape[1] <= 4096
        and frames.shape[1] > STEP and lone
    )


def solution(mesh):
    placed = (
        P(("half", "rows"), None),
        P(("half", "rows")),
        P(("half", "rows")),
        P("half", "rows"),
    )

    def run(frames, labels, counts, seeds):
        body = fused if fits(mesh, frames, seeds) else shards
        return jax.shard_map(
            body,
            mesh=mesh,
            in_specs=placed,
            out_specs=(P("half", "rows", None), P("half", "rows")),
            check_vma=False,
        )(frames, labels, counts, seeds)

    return run
```

```python
import functools
import math

import jax
import jax.numpy as jnp
from jax import lax
from jax.experimental import pallas as pl
from jax.experimental.pallas import tpu as pltpu
from jax.sharding import PartitionSpec as P


def from_partner(value, axis, stride):
    mask = 2**stride
    pairs = [(source, source ^ mask) for source in range(lax.axis_size(axis))]
    return lax.ppermute(value, axis, pairs)


def score_piece(rows_in, piece):
    cross = lax.dot_general(
        rows_in, piece, (((1,), (1,)), ((), ())), preferred_element_type=jnp.float32
    )
    wide = piece.astype(jnp.float32)
    return (cross - 0.5 * jnp.sum(wide * wide, axis=1)[None, :]) / math.sqrt(rows_in.shape[1])


def soft_weights(logits, valid):
    top = jnp.max(logits, axis=1, keepdims=True)
    expo = jnp.exp(logits - top)
    total = jnp.sum(expo, axis=1, keepdims=True)
    return (expo / total * valid[:, None]).astype(jnp.bfloat16)


def weighted(weights, rows_in):
    return lax.dot_general(
        weights, rows_in, (((0,), (0,)), ((), ())), preferred_element_type=jnp.float32
    )


def column_mass(weights):
    return jnp.sum(weights.astype(jnp.float32), axis=0)


def shards(frames, labels, counts, seeds):
    rows_dev = frames.shape[0]
    cap = rows_dev // 2
    side = lax.axis_index("half")
    spots = jnp.arange(rows_dev, dtype=jnp.int32)
    live = spots < counts[0]
    foreign = live & (labels != side)
    native = (live & (labels == side)).astype(jnp.float32)
    order = jnp.argsort(jnp.where(foreign, 0, 1).astype(jnp.int32), stable=True)
    picked = order[:cap]
    moved = frames[picked]
    flag = foreign[picked].astype(jnp.float32)
    mine = frames[seeds[0]]
    got_rows, got_flag = from_partner((moved, flag.astype(jnp.bfloat16)), "half", 0)
    pool = jnp.concatenate([frames, got_rows], axis=0)
    valid = jnp.concatenate([native, got_flag.astype(jnp.float32)])
    logits = score_piece(pool, lax.all_gather(mine, "rows", axis=0, tiled=True))
    weights = soft_weights(logits, valid)
    sums, mass = (
        lax.psum_scatter(weighted(weights, pool), "rows", scatter_dimension=0, tiled=True),
        lax.psum_scatter(column_mass(weights), "rows", scatter_dimension=0, tiled=True),
    )
    whole_k = mass.shape[0] * lax.axis_size("rows")
    total_slots = rows_dev * lax.axis_size("half") * lax.axis_size("rows")
    means = sums / (mass + 1.0)[:, None]
    occupancy = mass * (2.0 * whole_k / total_slots)
    return (means[None], occupancy[None])


MESH = pl.DeviceIdType.MESH
WIRE = jnp.bfloat16
STEP = 512
TILE = 16
EIGHT = 8
CHUNK = 256
EARLY = 0
PART = 128
LAG = 4
TURN = 1
BACK = 8
NT = (((1,), (1,)), ((), ()))
NN = (((1,), (0,)), ((), ()))


def round_up(value, unit):
    return -(-value // unit) * unit


def dot(a, b, how):
    return lax.dot_general(a, b, how, preferred_element_type=jnp.float32)


def column_weights(cross, norm, width, valid):
    logits = (cross - 0.5 * norm) / math.sqrt(width)
    top = jnp.max(logits, axis=0, keepdims=True)
    expo = jnp.exp(logits - top)
    total = jnp.sum(expo, axis=0, keepdims=True)
    return (expo / total * valid).astype(jnp.bfloat16)


def level(
    outer, width, scale,
    x_ref, odd_ref, labels_hbm, counts_ref, seeds_hbm,
    means_ref, occupancy_ref,
    labels_ref, seeds_ref, odd, xf, table, gone, came, squares, cross, near, weights,
    keep, csend, crecv, keepx, xsend, xrecv, zsend, zrecv,
    keept, zturn, zcame, xturn, xcame,
    small_load, x_load, y_out, y_in, u_out, d_out, t_out, t_in, c_out, c_in, x_out, x_in, z_out, z_in, zt_out, zt_in, xt_out, xt_in,
):
    slots = xf.shape[2]
    shard = seeds_ref.shape[1]
    steps = xf.shape[0]
    parts = gone.shape[0]
    sent = y_rows(width)
    whole = steps - 1
    rest = width - whole * STEP
    half_k = keep.shape[1]
    quarter_k = keepx.shape[1]
    side = lax.axis_index("half")
    row = lax.axis_index("rows")
    twin = row + 1 - 2 * (row % 2)
    across = row + 2 - 4 * ((row // 2) % 2)
    along = [
        ((row // 4 + d) % outer) * 4 + row % 4 for d in range(1, outer)
    ]

    even = rest // TILE * TILE

    def load(c):
        if isinstance(c, int) and c == whole:
            at = pl.ds(whole * STEP, even)
            return pltpu.make_async_copy(x_ref.at[at], xf.at[c, pl.ds(0, even)], x_load.at[c])
        at = pl.ds(pl.multiple_of(c * STEP, STEP), STEP)
        return pltpu.make_async_copy(x_ref.at[at], xf.at[c], x_load.at[c])

    labels_load = pltpu.make_async_copy(labels_hbm, labels_ref, small_load.at[0])
    seeds_load = pltpu.make_async_copy(seeds_hbm, seeds_ref, small_load.at[1])
    odd_load = pltpu.make_async_copy(odd_ref.at[width // EIGHT - 1], odd, small_load.at[2])
    labels_load.start()
    load(0).start()

    barrier = pltpu.get_barrier_semaphore()
    pl.semaphore_signal(barrier, inc=1, device_id=(1 - side, row), device_id_type=MESH)
    for peer in [twin, across] + along:
        pl.semaphore_signal(barrier, inc=1, device_id=(side, peer), device_id_type=MESH)

    def remote(src, dst, out_sem, in_sem, where):
        return pltpu.make_async_remote_copy(
            src_ref=src, dst_ref=dst, send_sem=out_sem, recv_sem=in_sem,
            device_id=where, device_id_type=MESH,
        )

    @pl.loop(1, whole)
    def _(c):
        load(c).start()

    load(whole).start()
    odd_load.start()
    seeds_load.start()
    spots = lax.broadcasted_iota(jnp.int32, (1, slots), 1)
    upper = (
        lax.broadcasted_iota(jnp.int32, (slots, slots), 0)
        <= lax.broadcasted_iota(jnp.int32, (slots, slots), 1)
    ).astype(jnp.float32).astype(jnp.bfloat16)
    live = spots < counts_ref[0]
    labels_load.wait()
    labels = labels_ref[...]
    native = (live & (labels == side)).astype(jnp.float32)
    foreign = jnp.where(live & (labels != side), 1.0, 0.0)
    rank = dot(jnp.broadcast_to(foreign, (16, slots)).astype(jnp.bfloat16), upper, NN)[:1]
    place = jnp.where(foreign > 0, rank - 1.0, -1.0).astype(jnp.int32)

    def pick(part):
        lane = lax.broadcasted_iota(jnp.int32, (PART, slots), 0) + part * PART
        return (lane == place).astype(jnp.float32).astype(jnp.bfloat16)

    def y_copy(part, c, rows=STEP):
        at = pl.ds(c * STEP, rows)
        return remote(
            gone.at[part, at], came.at[part, at],
            y_out.at[part, c], y_in.at[part, c], (1 - side, row),
        )

    last_rows = sent - whole * STEP

    def each_y(part, act):
        @pl.loop(0, whole)
        def _(c):
            act(y_copy(part, c))

        act(y_copy(part, whole, last_rows))

    first = pick(0)

    def leave(c):
        at = pl.ds(pl.multiple_of(c * STEP, STEP), STEP)
        load(c).wait()
        gone[0, at, :] = dot(xf[c], first, NT).astype(jnp.bfloat16)

    for c in range(EARLY):
        leave(c)
    pl.semaphore_wait(barrier, outer + 2)
    for c in range(EARLY):
        y_copy(0, c).start()

    @pl.loop(EARLY, whole)
    def _(c):
        leave(c)
        y_copy(0, c).start()

    load(whole).wait()
    odd_load.wait()
    ones = lax.broadcasted_iota(jnp.int32, (STEP - even, slots), 0) == rest - even
    fill = ones.astype(jnp.float32)
    if rest > even:
        fill = jnp.concatenate([odd[...].astype(jnp.float32), fill[rest - even :]], axis=0)
    xf[whole, pl.ds(even, STEP - even), :] = fill.astype(jnp.bfloat16)

    gone[0, pl.ds(whole * STEP, STEP), :] = dot(xf[whole], first, NT).astype(jnp.bfloat16)
    y_copy(0, whole, last_rows).start()

    seeds_load.wait()
    seeds = jnp.broadcast_to(seeds_ref[...], (shard, shard))
    diagonal = lax.broadcasted_iota(jnp.int32, (shard, shard), 0) == lax.broadcasted_iota(
        jnp.int32, (shard, shard), 1
    )
    seed = jnp.sum(jnp.where(diagonal, seeds, 0), axis=1, keepdims=True)
    chosen = (
        lax.broadcasted_iota(jnp.int32, (shard, slots), 1) == seed
    ).astype(jnp.float32).astype(jnp.bfloat16)

    @pl.loop(0, steps)
    def _(c):
        at = pl.ds(pl.multiple_of(c * STEP, STEP), STEP)
        lane = lax.broadcasted_iota(jnp.int32, (shard, STEP), 1) + c * STEP
        mine = dot(chosen, xf[c], NT)
        table[pl.ds(0, shard), at] = jnp.where(lane < width, mine, 0.0).astype(jnp.bfloat16)

    def t_copy(index, source, target, where):
        return remote(
            table.at[pl.ds(source * shard, shard)], table.at[pl.ds(target * shard, shard)],
            t_out.at[index], t_in.at[target], (side, where),
        )

    def up_copy(k):
        where = lax.rem(row + 4, outer * 4)
        return remote(
            table.at[pl.ds((outer - k) % outer * shard, shard)],
            table.at[pl.ds((outer - k - 1) * shard, shard)],
            u_out.at[k], t_in.at[outer - k - 1], (side, where),
        )

    def down_copy(k):
        where = lax.rem(row + (outer - 1) * 4, outer * 4)
        return remote(
            table.at[pl.ds(k * shard, shard)], table.at[pl.ds((k + 1) * shard, shard)],
            d_out.at[k], t_in.at[k + 1], (side, where),
        )

    x_gather = [t_copy(s, s, outer + s, across) for s in range(outer)]
    c_gather = [t_copy(outer + s, s, 2 * outer + s, twin) for s in range(2 * outer)]
    depth = row // 4

    @pl.when(depth > 0)
    def _():
        down_copy(0).start()

    @pl.when(depth < outer - 1)
    def _():
        up_copy(0).start()

    x_gather[0].start()
    c_gather[0].start()

    for part in range(1, parts):
        later = pick(part)

        @pl.loop(0, steps)
        def _(c):
            at = pl.ds(pl.multiple_of(c * STEP, STEP), STEP)
            gone[part, at, :] = dot(xf[c], later, NT).astype(jnp.bfloat16)

        each_y(part, lambda copy: copy.start())
    if steps * STEP > sent:
        for part in range(parts):
            came[part, pl.ds(sent, steps * STEP - sent), :] = jnp.zeros(
                (steps * STEP - sent, PART), jnp.bfloat16
            )

    def arrived(slot):
        return t_copy(0, 0, slot, twin).wait_recv()

    def from_above(k):
        arrived(k)

        @pl.when(depth > 0)
        def _():
            down_copy(k).start()

        x_gather[k].start()
        c_gather[k].start()

    def from_below(k):
        arrived(outer - k)

        @pl.when(depth < outer - 1)
        def _():
            up_copy(k).start()

        x_gather[outer - k].start()
        c_gather[outer - k].start()

    def crossed(s):
        x_gather[s].wait_recv()
        c_gather[outer + s].start()

    def both(k, above, below):
        @pl.when(depth + k <= outer - 1)
        def _():
            above(k)

        @pl.when(depth >= k)
        def _():
            below(k)

    for k in range(1, outer):
        both(k, from_above, from_below)
        if k == 1:
            crossed(0)
        else:
            both(k - 1, crossed, lambda back: crossed(outer - back))
    squares[...] = jnp.zeros_like(squares)
    near[...] = jnp.zeros_like(near)

    def score(group):
        rows_at = pl.ds(group * quarter_k, quarter_k)

        @pl.loop(0, steps)
        def _(c):
            at = pl.ds(pl.multiple_of(c * STEP, STEP), STEP)
            block = table[rows_at, at]
            near[rows_at, :] += dot(block, xf[c], NN)
            wide = block.astype(jnp.float32)
            wide = wide * wide
            total = wide[:, :PART]
            for lane in range(PART, STEP, PART):
                total += wide[:, lane : lane + PART]
            squares[rows_at, :] += total

    score(0)
    for s in range(outer):
        c_gather[s].wait_recv()
    score(2)
    both(outer - 1, crossed, lambda back: crossed(outer - back))
    score(1)
    for s in range(outer, 2 * outer):
        c_gather[s].wait_recv()
    score(3)

    norm = jnp.sum(squares[...], axis=1, keepdims=True)
    weights[:, pl.ds(0, slots)] = column_weights(near[...], norm, width, native)

    for part in range(parts):
        cross[...] = jnp.zeros_like(cross)

        @pl.loop(0, steps)
        def _(c):
            @pl.when(c < whole)
            def _():
                y_copy(part, c).wait_recv()

            @pl.when(c == whole)
            def _():
                y_copy(part, whole, last_rows).wait_recv()

            at = pl.ds(pl.multiple_of(c * STEP, STEP), STEP)
            cross[...] += dot(table[:, at], came[part, at, :], NN)

        flag = came[part, pl.ds(width // 16 * 16, 16), :].astype(jnp.float32)
        flag = flag[width % 16 : width % 16 + 1]
        weights[:, pl.ds(slots + part * PART, PART)] = column_weights(
            cross[...], norm, width, flag
        )

    last = width % CHUNK
    chunks = width // CHUNK + 1

    def column(c):
        return pl.multiple_of(lax.rem(c + chunks - 1, chunks) * CHUNK, CHUNK)

    def narrow(c, ref, sums):
        ref[...] = sums.astype(WIRE)

        @pl.when(c == 0)
        def _():
            low = last // PART * PART
            tile = sums[:, low : low + PART]
            lost = pltpu.roll(tile - tile.astype(WIRE).astype(jnp.float32), 1, 1)
            lane = lax.broadcasted_iota(jnp.int32, tile.shape, 1)
            tile = jnp.where(lane == last - low + 1, tile + lost, tile)
            ref[:, low : low + PART] = tile.astype(WIRE)

    def c_copy(c):
        return remote(csend.at[c], crecv.at[c], c_out.at[c], c_in.at[c], (side, twin))

    def x_copy(c):
        return remote(xsend.at[c], xrecv.at[c], x_out.at[c], x_in.at[c], (side, across))

    def z_copy(c, d):
        return remote(
            zsend.at[c, d - 1], zrecv.at[c, d - 1],
            z_out.at[c, d - 1], z_in.at[c, d - 1], (side, along[d - 1]),
        )

    def add_up(c):
        place = column(c)
        at = pl.ds(place, CHUNK)
        within = pl.ds(pl.multiple_of(place % STEP, CHUNK), CHUNK)
        block = jnp.concatenate(
            [xf[place // STEP, within]] + [came[part, at, :] for part in range(parts)], axis=1
        )
        sums = dot(weights[...], block, NT)
        csend[c] = sums[half_k:]
        c_copy(c).start()
        keep[c] = sums[:half_k]

    def zt_copy(d):
        return remote(
            zturn.at[d - 1], zcame.at[d - 1], zt_out.at[d - 1], zt_in.at[d - 1],
            (side, along[d - 1]),
        )

    def xt_copy():
        return remote(xturn, xcame, xt_out.at[0], xt_in.at[0], (side, across))

    def turn_along(c):
        c_copy(c).wait_recv()
        sums = keep[c] + crecv[c]
        for d in range(1, outer):
            near_rows = sums[d * shard : (d + 1) * shard]
            far_rows = sums[quarter_k + d * shard : quarter_k + (d + 1) * shard]
            zturn[d - 1, pl.ds(0, shard), :] = near_rows.astype(WIRE)
            zturn[d - 1, pl.ds(shard, shard), :] = far_rows.astype(WIRE)
            zt_copy(d).start()
        keept[pl.ds(0, shard), :] = sums[:shard]
        keept[pl.ds(shard, shard), :] = sums[quarter_k : quarter_k + shard]

    def turn_across():
        sums = keept[...]
        for d in range(1, outer):
            zt_copy(d).wait_recv()
            sums += zcame[d - 1].astype(jnp.float32)
        xturn[...] = sums[shard:].astype(WIRE)
        xt_copy().start()
        keept[pl.ds(0, shard), :] = sums[:shard]

    def to_across(c):
        c_copy(c).wait_recv()
        sums = keep[c] + crecv[c]
        narrow(c, xsend.at[c], sums[quarter_k:])
        x_copy(c).start()
        keepx[c] = sums[:quarter_k]

    def to_along(c):
        x_copy(c).wait_recv()
        sums = keepx[c] + xrecv[c].astype(jnp.float32)
        for d in range(1, outer):
            narrow(c, zsend.at[c, d - 1], sums[d * shard : (d + 1) * shard])
        for d in range(1, outer):
            z_copy(c, d).start()
        keepx[c, pl.ds(0, shard), :] = sums[:shard]

    @pl.loop(0, chunks + LAG)
    def _(c):
        @pl.when(c < chunks)
        def _():
            add_up(c)

        @pl.when((c > 0) & (c <= chunks) & (c != TURN + 1))
        def _():
            to_across(c - 1)

        @pl.when(c == TURN + 1)
        def _():
            turn_along(TURN)

        @pl.when((c >= LAG) & (c != LAG + TURN))
        def _():
            to_along(c - LAG)

        @pl.when(c == min(BACK, chunks + LAG - 1))
        def _():
            turn_across()

    def total(c):
        sums = keepx[c, pl.ds(0, shard), :]
        for d in range(1, outer):
            z_copy(c, d).wait_recv()
            sums += zrecv[c, d - 1].astype(jnp.float32)
        return sums

    sums = total(0)
    mass = sums[:, last : last + 1] + sums[:, last + 1 : last + 2]
    means_ref[:, pl.ds(width - last, last)] = sums[:, :last] / (mass + 1.0)
    turned = jnp.sum(jnp.where(diagonal, mass, 0.0), axis=0, keepdims=True)
    occupancy_ref[...] = turned * scale

    xt_copy().wait_recv()
    sums = keept[pl.ds(0, shard), :] + xcame[...].astype(jnp.float32)
    means_ref[:, pl.ds(column(TURN), CHUNK)] = sums / (mass + 1.0)

    @pl.loop(TURN + 1, chunks)
    def _(c):
        means_ref[:, pl.ds(column(c), CHUNK)] = total(c) / (mass + 1.0)

    for copy in x_gather + c_gather:
        copy.wait_send()
    for k in range(outer - 1):
        @pl.when((depth > 0) & (depth + k <= outer - 1))
        def _():
            down_copy(k).wait_send()

        @pl.when((depth < outer - 1) & (depth >= k))
        def _():
            up_copy(k).wait_send()

    for part in range(parts):
        each_y(part, lambda copy: copy.wait_send())

    @pl.loop(0, chunks)
    def _(c):
        c_copy(c).wait_send()

        @pl.when(c != TURN)
        def _():
            x_copy(c).wait_send()
            for d in range(1, outer):
                z_copy(c, d).wait_send()

    xt_copy().wait_send()
    for d in range(1, outer):
        zt_copy(d).wait_send()


def y_rows(width):
    return round_up(width + 1, 16)


def fused(frames, labels, counts, seeds):
    slots, width = frames.shape
    shard = seeds.shape[1]
    n_rows = lax.axis_size("rows")
    outer = n_rows // 4
    whole_k = shard * n_rows
    parts = slots // 2 // PART
    padded = round_up(width + 1, STEP)
    steps = padded // STEP
    chunks = width // CHUNK + 1
    total_slots = slots * lax.axis_size("half") * n_rows
    scale = 2.0 * whole_k / total_slots
    dma = pltpu.SemaphoreType.DMA
    bf16, f32 = jnp.bfloat16, jnp.float32
    flops = 4 * (slots + slots // 2) * whole_k * width
    vmem = pl.BlockSpec(memory_space=pltpu.VMEM)
    hbm = pl.BlockSpec(memory_space=pltpu.HBM)
    means, occupancy = pl.pallas_call(
        functools.partial(level, outer, width, scale),
        out_shape=(
            jax.ShapeDtypeStruct((shard, width), f32),
            jax.ShapeDtypeStruct((1, shard), f32),
        ),
        in_specs=[
            hbm,
            hbm, hbm, pl.BlockSpec(memory_space=pltpu.SMEM), hbm,
        ],
        out_specs=(vmem, vmem),
        scratch_shapes=[
            pltpu.VMEM((1, slots), jnp.int32),
            pltpu.VMEM((1, shard), jnp.int32),
            pltpu.VMEM((EIGHT, slots), bf16),
            pltpu.VMEM((steps, STEP, slots), bf16),
            pltpu.VMEM((whole_k, padded), bf16),
            pltpu.VMEM((parts, padded, PART), bf16),
            pltpu.VMEM((parts, padded, PART), bf16),
            pltpu.VMEM((whole_k, PART), f32),
            pltpu.VMEM((whole_k, PART), f32),
            pltpu.VMEM((whole_k, slots), f32),
            pltpu.VMEM((whole_k, slots + parts * PART), bf16),
            pltpu.VMEM((chunks, whole_k // 2, CHUNK), f32),
            pltpu.VMEM((chunks, whole_k // 2, CHUNK), f32),
            pltpu.VMEM((chunks, whole_k // 2, CHUNK), f32),
            pltpu.VMEM((chunks, whole_k // 4, CHUNK), f32),
            pltpu.VMEM((chunks, whole_k // 4, CHUNK), WIRE),
            pltpu.VMEM((chunks, whole_k // 4, CHUNK), WIRE),
            pltpu.VMEM((chunks, outer - 1, shard, CHUNK), WIRE),
            pltpu.VMEM((chunks, outer - 1, shard, CHUNK), WIRE),
            pltpu.VMEM((2 * shard, CHUNK), f32),
            pltpu.VMEM((outer - 1, 2 * shard, CHUNK), WIRE),
            pltpu.VMEM((outer - 1, 2 * shard, CHUNK), WIRE),
            pltpu.VMEM((shard, CHUNK), WIRE),
            pltpu.VMEM((shard, CHUNK), WIRE),
            dma((3,)), dma((steps,)), dma((parts, steps)), dma((parts, steps)),
            dma((outer,)), dma((outer,)),
            dma((4 * outer,)), dma((4 * outer,)),
            dma((chunks,)), dma((chunks,)),
            dma((chunks,)), dma((chunks,)),
            dma((chunks, outer - 1)), dma((chunks, outer - 1)),
            dma((outer - 1,)), dma((outer - 1,)), dma((1,)), dma((1,)),
        ],
        compiler_params=pltpu.CompilerParams(
            collective_id=0, has_side_effects=True, vmem_limit_bytes=52 * 2**20
        ),
        cost_estimate=pl.CostEstimate(
            flops=flops, bytes_accessed=slots * width * 2, transcendentals=slots * whole_k
        ),
    )(
        frames.T, frames.T.reshape(width // EIGHT, EIGHT, slots),
        pltpu.with_memory_space_constraint(labels[None], pltpu.HBM), counts,
        pltpu.with_memory_space_constraint(seeds, pltpu.HBM),
    )
    return (means[None], occupancy)


def fits(mesh, frames, seeds):
    sizes = dict(mesh.shape)
    n_half, n_rows = sizes["half"], sizes["rows"]
    slots = frames.shape[0] // (n_half * n_rows)
    shard = seeds.shape[1] // n_rows
    lone = frames.shape[1] % EIGHT == 0 and frames.shape[1] % STEP > 0 and frames.shape[1] % PART < PART - 1
    return (
        n_half == 2 and n_rows % 4 == 0 and n_rows >= 8 and shard % 16 == 0 and shard > 0
        and slots % (2 * PART) == 0 and slots * n_half * n_rows == frames.shape[0]
        and slots <= 1024 and seeds.shape[1] <= 512 and frames.shape[1] <= 4096
        and frames.shape[1] > STEP and lone
    )


def solution(mesh):
    placed = (
        P(("half", "rows"), None),
        P(("half", "rows")),
        P(("half", "rows")),
        P("half", "rows"),
    )

    def run(frames, labels, counts, seeds):
        body = fused if fits(mesh, frames, seeds) else shards
        return jax.shard_map(
            body,
            mesh=mesh,
            in_specs=placed,
            out_specs=(P("half", "rows", None), P("half", "rows")),
            check_vma=False,
        )(frames, labels, counts, seeds)

    return run
```

```python
import functools
import math

import jax
import jax.numpy as jnp
from jax import lax
from jax.experimental import pallas as pl
from jax.experimental.pallas import tpu as pltpu
from jax.sharding import PartitionSpec as P


def from_partner(value, axis, stride):
    mask = 2**stride
    pairs = [(source, source ^ mask) for source in range(lax.axis_size(axis))]
    return lax.ppermute(value, axis, pairs)


def score_piece(rows_in, piece):
    cross = lax.dot_general(
        rows_in, piece, (((1,), (1,)), ((), ())), preferred_element_type=jnp.float32
    )
    wide = piece.astype(jnp.float32)
    return (cross - 0.5 * jnp.sum(wide * wide, axis=1)[None, :]) / math.sqrt(rows_in.shape[1])


def soft_weights(logits, valid):
    top = jnp.max(logits, axis=1, keepdims=True)
    expo = jnp.exp(logits - top)
    total = jnp.sum(expo, axis=1, keepdims=True)
    return (expo / total * valid[:, None]).astype(jnp.bfloat16)


def weighted(weights, rows_in):
    return lax.dot_general(
        weights, rows_in, (((0,), (0,)), ((), ())), preferred_element_type=jnp.float32
    )


def column_mass(weights):
    return jnp.sum(weights.astype(jnp.float32), axis=0)


def shards(frames, labels, counts, seeds):
    rows_dev = frames.shape[0]
    cap = rows_dev // 2
    side = lax.axis_index("half")
    spots = jnp.arange(rows_dev, dtype=jnp.int32)
    live = spots < counts[0]
    foreign = live & (labels != side)
    native = (live & (labels == side)).astype(jnp.float32)
    order = jnp.argsort(jnp.where(foreign, 0, 1).astype(jnp.int32), stable=True)
    picked = order[:cap]
    moved = frames[picked]
    flag = foreign[picked].astype(jnp.float32)
    mine = frames[seeds[0]]
    got_rows, got_flag = from_partner((moved, flag.astype(jnp.bfloat16)), "half", 0)
    pool = jnp.concatenate([frames, got_rows], axis=0)
    valid = jnp.concatenate([native, got_flag.astype(jnp.float32)])
    logits = score_piece(pool, lax.all_gather(mine, "rows", axis=0, tiled=True))
    weights = soft_weights(logits, valid)
    sums, mass = (
        lax.psum_scatter(weighted(weights, pool), "rows", scatter_dimension=0, tiled=True),
        lax.psum_scatter(column_mass(weights), "rows", scatter_dimension=0, tiled=True),
    )
    whole_k = mass.shape[0] * lax.axis_size("rows")
    total_slots = rows_dev * lax.axis_size("half") * lax.axis_size("rows")
    means = sums / (mass + 1.0)[:, None]
    occupancy = mass * (2.0 * whole_k / total_slots)
    return (means[None], occupancy[None])


MESH = pl.DeviceIdType.MESH
WIRE = jnp.bfloat16
STEP = 512
TILE = 16
EIGHT = 8
CHUNK = 256
EARLY = 1
AHEAD = 3
PART = 128
LAG = 4
TURN = 1
BACK = 8
NT = (((1,), (1,)), ((), ()))
NN = (((1,), (0,)), ((), ()))


def round_up(value, unit):
    return -(-value // unit) * unit


def dot(a, b, how):
    return lax.dot_general(a, b, how, preferred_element_type=jnp.float32)


def column_weights(cross, norm, width, valid):
    logits = (cross - 0.5 * norm) / math.sqrt(width)
    top = jnp.max(logits, axis=0, keepdims=True)
    expo = jnp.exp(logits - top)
    total = jnp.sum(expo, axis=0, keepdims=True)
    return (expo / total * valid).astype(jnp.bfloat16)


def level(
    outer, width, scale,
    x_ref, odd_ref, labels_hbm, counts_ref, seeds_hbm,
    means_ref, occupancy_ref,
    labels_ref, seeds_ref, odd, xf, table, gone, came, squares, cross, near, weights,
    keep, csend, crecv, keepx, xsend, xrecv, zsend, zrecv,
    keept, zturn, zcame, xturn, xcame,
    small_load, x_load, y_out, y_in, u_out, d_out, t_out, t_in, c_out, c_in, x_out, x_in, z_out, z_in, zt_out, zt_in, xt_out, xt_in,
):
    slots = xf.shape[2]
    shard = seeds_ref.shape[1]
    steps = xf.shape[0]
    parts = gone.shape[0]
    sent = y_rows(width)
    whole = steps - 1
    rest = width - whole * STEP
    half_k = keep.shape[1]
    quarter_k = keepx.shape[1]
    side = lax.axis_index("half")
    row = lax.axis_index("rows")
    twin = row + 1 - 2 * (row % 2)
    across = row + 2 - 4 * ((row // 2) % 2)
    along = [
        ((row // 4 + d) % outer) * 4 + row % 4 for d in range(1, outer)
    ]

    even = rest // TILE * TILE

    def load(c):
        if isinstance(c, int) and c == whole:
            at = pl.ds(whole * STEP, even)
            return pltpu.make_async_copy(x_ref.at[at], xf.at[c, pl.ds(0, even)], x_load.at[c])
        at = pl.ds(pl.multiple_of(c * STEP, STEP), STEP)
        return pltpu.make_async_copy(x_ref.at[at], xf.at[c], x_load.at[c])

    labels_load = pltpu.make_async_copy(labels_hbm, labels_ref, small_load.at[0])
    seeds_load = pltpu.make_async_copy(seeds_hbm, seeds_ref, small_load.at[1])
    odd_load = pltpu.make_async_copy(odd_ref.at[width // EIGHT - 1], odd, small_load.at[2])
    barrier = pltpu.get_barrier_semaphore()
    pl.semaphore_signal(barrier, inc=1, device_id=(1 - side, row), device_id_type=MESH)
    for peer in [twin, across] + along:
        pl.semaphore_signal(barrier, inc=1, device_id=(side, peer), device_id_type=MESH)

    labels_load.start()
    load(0).start()

    def remote(src, dst, out_sem, in_sem, where):
        return pltpu.make_async_remote_copy(
            src_ref=src, dst_ref=dst, send_sem=out_sem, recv_sem=in_sem,
            device_id=where, device_id_type=MESH,
        )

    @pl.loop(1, whole)
    def _(c):
        load(c).start()

    load(whole).start()
    odd_load.start()
    seeds_load.start()
    spots = lax.broadcasted_iota(jnp.int32, (1, slots), 1)
    upper = (
        lax.broadcasted_iota(jnp.int32, (slots, slots), 0)
        <= lax.broadcasted_iota(jnp.int32, (slots, slots), 1)
    ).astype(jnp.float32).astype(jnp.bfloat16)
    live = spots < counts_ref[0]
    labels_load.wait()
    labels = labels_ref[...]
    native = (live & (labels == side)).astype(jnp.float32)
    foreign = jnp.where(live & (labels != side), 1.0, 0.0)
    rank = dot(jnp.broadcast_to(foreign, (16, slots)).astype(jnp.bfloat16), upper, NN)[:1]
    place = jnp.where(foreign > 0, rank - 1.0, -1.0).astype(jnp.int32)

    def pick(part):
        lane = lax.broadcasted_iota(jnp.int32, (PART, slots), 0) + part * PART
        return (lane == place).astype(jnp.float32).astype(jnp.bfloat16)

    def y_copy(part, c, rows=STEP):
        at = pl.ds(c * STEP, rows)
        return remote(
            gone.at[part, at], came.at[part, at],
            y_out.at[part, c], y_in.at[part, c], (1 - side, row),
        )

    last_rows = sent - whole * STEP

    def each_y(part, act):
        @pl.loop(0, whole)
        def _(c):
            act(y_copy(part, c))

        act(y_copy(part, whole, last_rows))

    first = pick(0)

    def leave(c):
        at = pl.ds(pl.multiple_of(c * STEP, STEP), STEP)
        load(c).wait()
        gone[0, at, :] = dot(xf[c], first, NT).astype(jnp.bfloat16)

    for c in range(EARLY):
        leave(c)
    pl.semaphore_wait(barrier, outer + 2)
    for c in range(EARLY):
        y_copy(0, c).start()

    @pl.loop(EARLY, whole)
    def _(c):
        leave(c)
        y_copy(0, c).start()

    load(whole).wait()
    odd_load.wait()
    ones = lax.broadcasted_iota(jnp.int32, (STEP - even, slots), 0) == rest - even
    fill = ones.astype(jnp.float32)
    if rest > even:
        fill = jnp.concatenate([odd[...].astype(jnp.float32), fill[rest - even :]], axis=0)
    xf[whole, pl.ds(even, STEP - even), :] = fill.astype(jnp.bfloat16)

    gone[0, pl.ds(whole * STEP, STEP), :] = dot(xf[whole], first, NT).astype(jnp.bfloat16)
    y_copy(0, whole, last_rows).start()

    seeds_load.wait()
    seeds = jnp.broadcast_to(seeds_ref[...], (shard, shard))
    diagonal = lax.broadcasted_iota(jnp.int32, (shard, shard), 0) == lax.broadcasted_iota(
        jnp.int32, (shard, shard), 1
    )
    seed = jnp.sum(jnp.where(diagonal, seeds, 0), axis=1, keepdims=True)
    chosen = (
        lax.broadcasted_iota(jnp.int32, (shard, slots), 1) == seed
    ).astype(jnp.float32).astype(jnp.bfloat16)

    @pl.loop(0, steps)
    def _(c):
        at = pl.ds(pl.multiple_of(c * STEP, STEP), STEP)
        lane = lax.broadcasted_iota(jnp.int32, (shard, STEP), 1) + c * STEP
        mine = dot(chosen, xf[c], NT)
        table[pl.ds(0, shard), at] = jnp.where(lane < width, mine, 0.0).astype(jnp.bfloat16)

    def t_copy(index, source, target, where):
        return remote(
            table.at[pl.ds(source * shard, shard)], table.at[pl.ds(target * shard, shard)],
            t_out.at[index], t_in.at[target], (side, where),
        )

    def up_copy(k):
        where = lax.rem(row + 4, outer * 4)
        return remote(
            table.at[pl.ds((outer - k) % outer * shard, shard)],
            table.at[pl.ds((outer - k - 1) * shard, shard)],
            u_out.at[k], t_in.at[outer - k - 1], (side, where),
        )

    def down_copy(k):
        where = lax.rem(row + (outer - 1) * 4, outer * 4)
        return remote(
            table.at[pl.ds(k * shard, shard)], table.at[pl.ds((k + 1) * shard, shard)],
            d_out.at[k], t_in.at[k + 1], (side, where),
        )

    x_gather = [t_copy(s, s, outer + s, across) for s in range(outer)]
    c_gather = [t_copy(outer + s, s, 2 * outer + s, twin) for s in range(2 * outer)]
    depth = row // 4

    @pl.when(depth > 0)
    def _():
        down_copy(0).start()

    @pl.when(depth < outer - 1)
    def _():
        up_copy(0).start()

    x_gather[0].start()
    c_gather[0].start()

    for part in range(1, parts):
        later = pick(part)

        @pl.loop(0, steps)
        def _(c):
            at = pl.ds(pl.multiple_of(c * STEP, STEP), STEP)
            gone[part, at, :] = dot(xf[c], later, NT).astype(jnp.bfloat16)

        each_y(part, lambda copy: copy.start())
    if steps * STEP > sent:
        for part in range(parts):
            came[part, pl.ds(sent, steps * STEP - sent), :] = jnp.zeros(
                (steps * STEP - sent, PART), jnp.bfloat16
            )

    def arrived(slot):
        return t_copy(0, 0, slot, twin).wait_recv()

    def from_above(k):
        arrived(k)

        @pl.when(depth > 0)
        def _():
            down_copy(k).start()

        x_gather[k].start()
        c_gather[k].start()

    def from_below(k):
        arrived(outer - k)

        @pl.when(depth < outer - 1)
        def _():
            up_copy(k).start()

        x_gather[outer - k].start()
        c_gather[outer - k].start()

    def crossed(s):
        x_gather[s].wait_recv()
        c_gather[outer + s].start()

    def both(k, above, below):
        @pl.when(depth + k <= outer - 1)
        def _():
            above(k)

        @pl.when(depth >= k)
        def _():
            below(k)

    for k in range(1, outer):
        both(k, from_above, from_below)
        if k == 1:
            crossed(0)
        else:
            both(k - 1, crossed, lambda back: crossed(outer - back))
    squares[...] = jnp.zeros_like(squares)
    near[...] = jnp.zeros_like(near)

    def score(group):
        rows_at = pl.ds(group * quarter_k, quarter_k)

        @pl.loop(0, steps)
        def _(c):
            at = pl.ds(pl.multiple_of(c * STEP, STEP), STEP)
            block = table[rows_at, at]
            near[rows_at, :] += dot(block, xf[c], NN)
            wide = block.astype(jnp.float32)
            wide = wide * wide
            total = wide[:, :PART]
            for lane in range(PART, STEP, PART):
                total += wide[:, lane : lane + PART]
            squares[rows_at, :] += total

    score(0)
    for s in range(outer):
        c_gather[s].wait_recv()
    score(2)
    both(outer - 1, crossed, lambda back: crossed(outer - back))
    score(1)
    for s in range(outer, 2 * outer):
        c_gather[s].wait_recv()
    score(3)

    norm = jnp.sum(squares[...], axis=1, keepdims=True)
    weights[:, pl.ds(0, slots)] = column_weights(near[...], norm, width, native)

    last = width % CHUNK
    chunks = width // CHUNK + 1

    def column(c):
        return pl.multiple_of(lax.rem(c + chunks - 1, chunks) * CHUNK, CHUNK)

    def weigh(c, parts_in, native_in):
        place = column(c)
        at = pl.ds(place, CHUNK)
        within = pl.ds(pl.multiple_of(place % STEP, CHUNK), CHUNK)
        block = [xf[place // STEP, within]] if native_in else []
        block += [came[part, at, :] for part in parts_in]
        first_lane = 0 if native_in else slots + parts_in[0] * PART
        count = (slots if native_in else 0) + len(parts_in) * PART
        return dot(
            weights[:, pl.ds(first_lane, count)],
            block[0] if len(block) == 1 else jnp.concatenate(block, axis=1), NT,
        )

    def begin_sums():
        @pl.loop(0, AHEAD)
        def _(c):
            sums = weigh(c, list(range(parts - 1)), True)
            csend[c] = sums[half_k:]
            keep[c] = sums[:half_k]

    for part in range(parts):
        if part == parts - 1:
            begin_sums()
        cross[...] = jnp.zeros_like(cross)

        @pl.loop(0, steps)
        def _(c):
            @pl.when(c < whole)
            def _():
                y_copy(part, c).wait_recv()

            @pl.when(c == whole)
            def _():
                y_copy(part, whole, last_rows).wait_recv()

            at = pl.ds(pl.multiple_of(c * STEP, STEP), STEP)
            cross[...] += dot(table[:, at], came[part, at, :], NN)

        flag = came[part, pl.ds(width // 16 * 16, 16), :].astype(jnp.float32)
        flag = flag[width % 16 : width % 16 + 1]
        weights[:, pl.ds(slots + part * PART, PART)] = column_weights(
            cross[...], norm, width, flag
        )

    def narrow(c, ref, sums):
        ref[...] = sums.astype(WIRE)

        @pl.when(c == 0)
        def _():
            low = last // PART * PART
            tile = sums[:, low : low + PART]
            lost = pltpu.roll(tile - tile.astype(WIRE).astype(jnp.float32), 1, 1)
            lane = lax.broadcasted_iota(jnp.int32, tile.shape, 1)
            tile = jnp.where(lane == last - low + 1, tile + lost, tile)
            ref[:, low : low + PART] = tile.astype(WIRE)

    def c_copy(c):
        return remote(csend.at[c], crecv.at[c], c_out.at[c], c_in.at[c], (side, twin))

    def x_copy(c):
        return remote(xsend.at[c], xrecv.at[c], x_out.at[c], x_in.at[c], (side, across))

    def z_copy(c, d):
        return remote(
            zsend.at[c, d - 1], zrecv.at[c, d - 1],
            z_out.at[c, d - 1], z_in.at[c, d - 1], (side, along[d - 1]),
        )

    def add_up(c):
        @pl.when(c < AHEAD)
        def _():
            sums = weigh(c, [parts - 1], False)
            csend[c] += sums[half_k:]
            c_copy(c).start()
            keep[c] += sums[:half_k]

        @pl.when(c >= AHEAD)
        def _():
            sums = weigh(c, list(range(parts)), True)
            csend[c] = sums[half_k:]
            c_copy(c).start()
            keep[c] = sums[:half_k]

    def zt_copy(d):
        return remote(
            zturn.at[d - 1], zcame.at[d - 1], zt_out.at[d - 1], zt_in.at[d - 1],
            (side, along[d - 1]),
        )

    def xt_copy():
        return remote(xturn, xcame, xt_out.at[0], xt_in.at[0], (side, across))

    def turn_along(c):
        c_copy(c).wait_recv()
        sums = keep[c] + crecv[c]
        for d in range(1, outer):
            near_rows = sums[d * shard : (d + 1) * shard]
            far_rows = sums[quarter_k + d * shard : quarter_k + (d + 1) * shard]
            zturn[d - 1, pl.ds(0, shard), :] = near_rows.astype(WIRE)
            zturn[d - 1, pl.ds(shard, shard), :] = far_rows.astype(WIRE)
            zt_copy(d).start()
        keept[pl.ds(0, shard), :] = sums[:shard]
        keept[pl.ds(shard, shard), :] = sums[quarter_k : quarter_k + shard]

    def turn_across():
        sums = keept[...]
        for d in range(1, outer):
            zt_copy(d).wait_recv()
            sums += zcame[d - 1].astype(jnp.float32)
        xturn[...] = sums[shard:].astype(WIRE)
        xt_copy().start()
        keept[pl.ds(0, shard), :] = sums[:shard]

    def to_across(c):
        c_copy(c).wait_recv()
        sums = keep[c] + crecv[c]
        narrow(c, xsend.at[c], sums[quarter_k:])
        x_copy(c).start()
        keepx[c] = sums[:quarter_k]

    def to_along(c):
        x_copy(c).wait_recv()
        sums = keepx[c] + xrecv[c].astype(jnp.float32)
        for d in range(1, outer):
            narrow(c, zsend.at[c, d - 1], sums[d * shard : (d + 1) * shard])
        for d in range(1, outer):
            z_copy(c, d).start()
        keepx[c, pl.ds(0, shard), :] = sums[:shard]

    @pl.loop(0, chunks + 1)
    def _(c):
        @pl.when(c < chunks)
        def _():
            add_up(c)

        @pl.when((c > 0) & (c <= chunks) & (c != TURN + 1))
        def _():
            to_across(c - 1)

        @pl.when(c == TURN + 1)
        def _():
            turn_along(TURN)

        @pl.when((c >= LAG) & (c != LAG + TURN))
        def _():
            to_along(c - LAG)

        @pl.when(c == BACK)
        def _():
            turn_across()

    def total(c):
        sums = keepx[c, pl.ds(0, shard), :]
        for d in range(1, outer):
            z_copy(c, d).wait_recv()
            sums += zrecv[c, d - 1].astype(jnp.float32)
        return sums

    def finish(c):
        means_ref[:, pl.ds(column(c), CHUNK)] = total(c) / (mass + 1.0)
        sent_chunk(c)

    def sent_chunk(c):
        c_copy(c).wait_send()
        x_copy(c).wait_send()
        for d in range(1, outer):
            z_copy(c, d).wait_send()

    sums = total(0)
    mass = sums[:, last : last + 1] + sums[:, last + 1 : last + 2]
    means_ref[:, pl.ds(width - last, last)] = sums[:, :last] / (mass + 1.0)
    turned = jnp.sum(jnp.where(diagonal, mass, 0.0), axis=0, keepdims=True)
    occupancy_ref[...] = turned * scale
    sent_chunk(0)
    pl.loop(TURN + 1, TURN + 3)(finish)
    to_along(chunks - 3)

    xt_copy().wait_recv()
    sums = keept[pl.ds(0, shard), :] + xcame[...].astype(jnp.float32)
    means_ref[:, pl.ds(column(TURN), CHUNK)] = sums / (mass + 1.0)
    c_copy(TURN).wait_send()
    xt_copy().wait_send()
    for d in range(1, outer):
        zt_copy(d).wait_send()
    for copy in x_gather + c_gather:
        copy.wait_send()
    for k in range(outer - 1):
        @pl.when((depth > 0) & (depth + k <= outer - 1))
        def _():
            down_copy(k).wait_send()

        @pl.when((depth < outer - 1) & (depth >= k))
        def _():
            up_copy(k).wait_send()

    to_along(chunks - 2)
    for part in range(parts):
        each_y(part, lambda copy: copy.wait_send())
    pl.loop(TURN + 3, TURN + 5)(finish)
    to_along(chunks - 1)
    pl.loop(TURN + 5, chunks)(finish)


def y_rows(width):
    return round_up(width + 1, 16)


def fused(frames, labels, counts, seeds):
    slots, width = frames.shape
    shard = seeds.shape[1]
    n_rows = lax.axis_size("rows")
    outer = n_rows // 4
    whole_k = shard * n_rows
    parts = slots // 2 // PART
    padded = round_up(width + 1, STEP)
    steps = padded // STEP
    chunks = width // CHUNK + 1
    total_slots = slots * lax.axis_size("half") * n_rows
    scale = 2.0 * whole_k / total_slots
    dma = pltpu.SemaphoreType.DMA
    bf16, f32 = jnp.bfloat16, jnp.float32
    flops = 4 * (slots + slots // 2) * whole_k * width
    vmem = pl.BlockSpec(memory_space=pltpu.VMEM)
    hbm = pl.BlockSpec(memory_space=pltpu.HBM)
    means, occupancy = pl.pallas_call(
        functools.partial(level, outer, width, scale),
        out_shape=(
            jax.ShapeDtypeStruct((shard, width), f32),
            jax.ShapeDtypeStruct((1, shard), f32),
        ),
        in_specs=[
            hbm,
            hbm, hbm, pl.BlockSpec(memory_space=pltpu.SMEM), hbm,
        ],
        out_specs=(vmem, vmem),
        scratch_shapes=[
            pltpu.VMEM((1, slots), jnp.int32),
            pltpu.VMEM((1, shard), jnp.int32),
            pltpu.VMEM((EIGHT, slots), bf16),
            pltpu.VMEM((steps, STEP, slots), bf16),
            pltpu.VMEM((whole_k, padded), bf16),
            pltpu.VMEM((parts, padded, PART), bf16),
            pltpu.VMEM((parts, padded, PART), bf16),
            pltpu.VMEM((whole_k, PART), f32),
            pltpu.VMEM((whole_k, PART), f32),
            pltpu.VMEM((whole_k, slots), f32),
            pltpu.VMEM((whole_k, slots + parts * PART), bf16),
            pltpu.VMEM((chunks, whole_k // 2, CHUNK), f32),
            pltpu.VMEM((chunks, whole_k // 2, CHUNK), f32),
            pltpu.VMEM((chunks, whole_k // 2, CHUNK), f32),
            pltpu.VMEM((chunks, whole_k // 4, CHUNK), f32),
            pltpu.VMEM((chunks, whole_k // 4, CHUNK), WIRE),
            pltpu.VMEM((chunks, whole_k // 4, CHUNK), WIRE),
            pltpu.VMEM((chunks, outer - 1, shard, CHUNK), WIRE),
            pltpu.VMEM((chunks, outer - 1, shard, CHUNK), WIRE),
            pltpu.VMEM((2 * shard, CHUNK), f32),
            pltpu.VMEM((outer - 1, 2 * shard, CHUNK), WIRE),
            pltpu.VMEM((outer - 1, 2 * shard, CHUNK), WIRE),
            pltpu.VMEM((shard, CHUNK), WIRE),
            pltpu.VMEM((shard, CHUNK), WIRE),
            dma((3,)), dma((steps,)), dma((parts, steps)), dma((parts, steps)),
            dma((outer,)), dma((outer,)),
            dma((4 * outer,)), dma((4 * outer,)),
            dma((chunks,)), dma((chunks,)),
            dma((chunks,)), dma((chunks,)),
            dma((chunks, outer - 1)), dma((chunks, outer - 1)),
            dma((outer - 1,)), dma((outer - 1,)), dma((1,)), dma((1,)),
        ],
        compiler_params=pltpu.CompilerParams(
            collective_id=0, has_side_effects=True, vmem_limit_bytes=52 * 2**20
        ),
        cost_estimate=pl.CostEstimate(
            flops=flops, bytes_accessed=slots * width * 2, transcendentals=slots * whole_k
        ),
    )(
        frames.T, frames.T.reshape(width // EIGHT, EIGHT, slots),
        pltpu.with_memory_space_constraint(labels[None], pltpu.HBM), counts,
        pltpu.with_memory_space_constraint(seeds, pltpu.HBM),
    )
    return (means[None], occupancy)


def fits(mesh, frames, seeds):
    sizes = dict(mesh.shape)
    n_half, n_rows = sizes["half"], sizes["rows"]
    slots = frames.shape[0] // (n_half * n_rows)
    shard = seeds.shape[1] // n_rows
    lone = frames.shape[1] % EIGHT == 0 and frames.shape[1] % STEP > 0 and frames.shape[1] % PART < PART - 1
    return (
        n_half == 2 and n_rows % 4 == 0 and n_rows >= 8 and shard % 16 == 0 and shard > 0
        and slots % (2 * PART) == 0 and slots * n_half * n_rows == frames.shape[0]
        and slots <= 1024 and seeds.shape[1] <= 512 and frames.shape[1] <= 4096
        and frames.shape[1] // CHUNK >= max(BACK, TURN + 6) and lone
    )


def solution(mesh):
    placed = (
        P(("half", "rows"), None),
        P(("half", "rows")),
        P(("half", "rows")),
        P("half", "rows"),
    )

    def run(frames, labels, counts, seeds):
        body = fused if fits(mesh, frames, seeds) else shards
        return jax.shard_map(
            body,
            mesh=mesh,
            in_specs=placed,
            out_specs=(P("half", "rows", None), P("half", "rows")),
            check_vma=False,
        )(frames, labels, counts, seeds)

    return run
```

```python
import functools
import math

import jax
import jax.numpy as jnp
from jax import lax
from jax.experimental import pallas as pl
from jax.experimental.pallas import tpu as pltpu
from jax.sharding import PartitionSpec as P


def from_partner(value, axis, stride):
    mask = 2**stride
    pairs = [(source, source ^ mask) for source in range(lax.axis_size(axis))]
    return lax.ppermute(value, axis, pairs)


def score_piece(rows_in, piece):
    cross = lax.dot_general(
        rows_in, piece, (((1,), (1,)), ((), ())), preferred_element_type=jnp.float32
    )
    wide = piece.astype(jnp.float32)
    return (cross - 0.5 * jnp.sum(wide * wide, axis=1)[None, :]) / math.sqrt(rows_in.shape[1])


def soft_weights(logits, valid):
    top = jnp.max(logits, axis=1, keepdims=True)
    expo = jnp.exp(logits - top)
    total = jnp.sum(expo, axis=1, keepdims=True)
    return (expo / total * valid[:, None]).astype(jnp.bfloat16)


def weighted(weights, rows_in):
    return lax.dot_general(
        weights, rows_in, (((0,), (0,)), ((), ())), preferred_element_type=jnp.float32
    )


def column_mass(weights):
    return jnp.sum(weights.astype(jnp.float32), axis=0)


def shards(frames, labels, counts, seeds):
    rows_dev = frames.shape[0]
    cap = rows_dev // 2
    side = lax.axis_index("half")
    spots = jnp.arange(rows_dev, dtype=jnp.int32)
    live = spots < counts[0]
    foreign = live & (labels != side)
    native = (live & (labels == side)).astype(jnp.float32)
    order = jnp.argsort(jnp.where(foreign, 0, 1).astype(jnp.int32), stable=True)
    picked = order[:cap]
    moved = frames[picked]
    flag = foreign[picked].astype(jnp.float32)
    mine = frames[seeds[0]]
    got_rows, got_flag = from_partner((moved, flag.astype(jnp.bfloat16)), "half", 0)
    pool = jnp.concatenate([frames, got_rows], axis=0)
    valid = jnp.concatenate([native, got_flag.astype(jnp.float32)])
    logits = score_piece(pool, lax.all_gather(mine, "rows", axis=0, tiled=True))
    weights = soft_weights(logits, valid)
    sums, mass = (
        lax.psum_scatter(weighted(weights, pool), "rows", scatter_dimension=0, tiled=True),
        lax.psum_scatter(column_mass(weights), "rows", scatter_dimension=0, tiled=True),
    )
    whole_k = mass.shape[0] * lax.axis_size("rows")
    total_slots = rows_dev * lax.axis_size("half") * lax.axis_size("rows")
    means = sums / (mass + 1.0)[:, None]
    occupancy = mass * (2.0 * whole_k / total_slots)
    return (means[None], occupancy[None])


MESH = pl.DeviceIdType.MESH
WIRE = jnp.bfloat16
STEP = 512
TILE = 16
EIGHT = 8
CHUNK = 256
EARLY = 1
AHEAD = 3
PART = 128
LAG = 4
TURN = 1
BACK = 8
NT = (((1,), (1,)), ((), ()))
NN = (((1,), (0,)), ((), ()))


def round_up(value, unit):
    return -(-value // unit) * unit


def dot(a, b, how):
    return lax.dot_general(a, b, how, preferred_element_type=jnp.float32)


def column_weights(cross, norm, width, valid):
    logits = (cross - 0.5 * norm) / math.sqrt(width)
    top = jnp.max(logits, axis=0, keepdims=True)
    expo = jnp.exp(logits - top)
    total = jnp.sum(expo, axis=0, keepdims=True)
    return (expo / total * valid).astype(jnp.bfloat16)


def level(
    outer, width, scale,
    x_ref, odd_ref, labels_hbm, counts_ref, seeds_hbm,
    means_ref, occupancy_ref,
    labels_ref, seeds_ref, odd, xf, table, gone, came, squares, cross, near, weights,
    keep, csend, crecv, keepx, xsend, xrecv, zsend, zrecv,
    keept, zturn, zcame, xturn, xcame,
    small_load, x_load, y_out, y_in, u_out, d_out, t_out, t_in, c_out, c_in, x_out, x_in, z_out, z_in, zt_out, zt_in, xt_out, xt_in,
):
    slots = xf.shape[2]
    shard = seeds_ref.shape[1]
    steps = xf.shape[0]
    parts = gone.shape[0]
    sent = y_rows(width)
    whole = steps - 1
    rest = width - whole * STEP
    half_k = keep.shape[1]
    quarter_k = keepx.shape[1]
    side = lax.axis_index("half")
    row = lax.axis_index("rows")
    twin = row + 1 - 2 * (row % 2)
    across = row + 2 - 4 * ((row // 2) % 2)
    along = [
        ((row // 4 + d) % outer) * 4 + row % 4 for d in range(1, outer)
    ]

    even = rest // TILE * TILE

    def load(c):
        if isinstance(c, int) and c == whole:
            at = pl.ds(whole * STEP, even)
            return pltpu.make_async_copy(x_ref.at[at], xf.at[c, pl.ds(0, even)], x_load.at[c])
        at = pl.ds(pl.multiple_of(c * STEP, STEP), STEP)
        return pltpu.make_async_copy(x_ref.at[at], xf.at[c], x_load.at[c])

    labels_load = pltpu.make_async_copy(labels_hbm, labels_ref, small_load.at[0])
    seeds_load = pltpu.make_async_copy(seeds_hbm, seeds_ref, small_load.at[1])
    odd_load = pltpu.make_async_copy(odd_ref.at[width // EIGHT - 1], odd, small_load.at[2])
    barrier = pltpu.get_barrier_semaphore()
    pl.semaphore_signal(barrier, inc=1, device_id=(1 - side, row), device_id_type=MESH)
    for peer in [twin, across] + along:
        pl.semaphore_signal(barrier, inc=1, device_id=(side, peer), device_id_type=MESH)

    labels_load.start()
    load(0).start()

    def remote(src, dst, out_sem, in_sem, where):
        return pltpu.make_async_remote_copy(
            src_ref=src, dst_ref=dst, send_sem=out_sem, recv_sem=in_sem,
            device_id=where, device_id_type=MESH,
        )

    @pl.loop(1, whole)
    def _(c):
        load(c).start()

    load(whole).start()
    odd_load.start()
    seeds_load.start()
    spots = lax.broadcasted_iota(jnp.int32, (1, slots), 1)
    upper = (
        lax.broadcasted_iota(jnp.int32, (slots, slots), 0)
        <= lax.broadcasted_iota(jnp.int32, (slots, slots), 1)
    ).astype(jnp.float32).astype(jnp.bfloat16)
    live = spots < counts_ref[0]
    labels_load.wait()
    labels = labels_ref[...]
    native = (live & (labels == side)).astype(jnp.float32)
    foreign = jnp.where(live & (labels != side), 1.0, 0.0)
    rank = dot(jnp.broadcast_to(foreign, (16, slots)).astype(jnp.bfloat16), upper, NN)[:1]
    place = jnp.where(foreign > 0, rank - 1.0, -1.0).astype(jnp.int32)

    def pick(part):
        lane = lax.broadcasted_iota(jnp.int32, (PART, slots), 0) + part * PART
        return (lane == place).astype(jnp.float32).astype(jnp.bfloat16)

    def y_copy(part, c, rows=STEP):
        at = pl.ds(c * STEP, rows)
        return remote(
            gone.at[part, at], came.at[part, at],
            y_out.at[part, c], y_in.at[part, c], (1 - side, row),
        )

    last_rows = sent - whole * STEP

    def each_y(part, act):
        @pl.loop(0, whole)
        def _(c):
            act(y_copy(part, c))

        act(y_copy(part, whole, last_rows))

    first = pick(0)

    def leave(c):
        at = pl.ds(pl.multiple_of(c * STEP, STEP), STEP)
        load(c).wait()
        gone[0, at, :] = dot(xf[c], first, NT).astype(jnp.bfloat16)

    for c in range(EARLY):
        leave(c)
    pl.semaphore_wait(barrier, outer + 2)
    for c in range(EARLY):
        y_copy(0, c).start()

    @pl.loop(EARLY, whole)
    def _(c):
        leave(c)
        y_copy(0, c).start()

    load(whole).wait()
    odd_load.wait()
    ones = lax.broadcasted_iota(jnp.int32, (STEP - even, slots), 0) == rest - even
    fill = ones.astype(jnp.float32)
    if rest > even:
        fill = jnp.concatenate([odd[...].astype(jnp.float32), fill[rest - even :]], axis=0)
    xf[whole, pl.ds(even, STEP - even), :] = fill.astype(jnp.bfloat16)

    gone[0, pl.ds(whole * STEP, STEP), :] = dot(xf[whole], first, NT).astype(jnp.bfloat16)
    y_copy(0, whole, last_rows).start()

    seeds_load.wait()
    seeds = jnp.broadcast_to(seeds_ref[...], (shard, shard))
    diagonal = lax.broadcasted_iota(jnp.int32, (shard, shard), 0) == lax.broadcasted_iota(
        jnp.int32, (shard, shard), 1
    )
    seed = jnp.sum(jnp.where(diagonal, seeds, 0), axis=1, keepdims=True)
    chosen = (
        lax.broadcasted_iota(jnp.int32, (shard, slots), 1) == seed
    ).astype(jnp.float32).astype(jnp.bfloat16)

    @pl.loop(0, steps)
    def _(c):
        at = pl.ds(pl.multiple_of(c * STEP, STEP), STEP)
        lane = lax.broadcasted_iota(jnp.int32, (shard, STEP), 1) + c * STEP
        mine = dot(chosen, xf[c], NT)
        table[pl.ds(0, shard), at] = jnp.where(lane < width, mine, 0.0).astype(jnp.bfloat16)

    def t_copy(index, source, target, where):
        return remote(
            table.at[pl.ds(source * shard, shard)], table.at[pl.ds(target * shard, shard)],
            t_out.at[index], t_in.at[target], (side, where),
        )

    def up_copy(k):
        where = lax.rem(row + 4, outer * 4)
        return remote(
            table.at[pl.ds((outer - k) % outer * shard, shard)],
            table.at[pl.ds((outer - k - 1) * shard, shard)],
            u_out.at[k], t_in.at[outer - k - 1], (side, where),
        )

    def down_copy(k):
        where = lax.rem(row + (outer - 1) * 4, outer * 4)
        return remote(
            table.at[pl.ds(k * shard, shard)], table.at[pl.ds((k + 1) * shard, shard)],
            d_out.at[k], t_in.at[k + 1], (side, where),
        )

    x_gather = [t_copy(s, s, outer + s, across) for s in range(outer)]
    c_gather = [t_copy(outer + s, s, 2 * outer + s, twin) for s in range(2 * outer)]
    depth = row // 4

    @pl.when(depth > 0)
    def _():
        down_copy(0).start()

    @pl.when(depth < outer - 1)
    def _():
        up_copy(0).start()

    x_gather[0].start()
    c_gather[0].start()

    for part in range(1, parts):
        later = pick(part)

        @pl.loop(0, steps)
        def _(c):
            at = pl.ds(pl.multiple_of(c * STEP, STEP), STEP)
            gone[part, at, :] = dot(xf[c], later, NT).astype(jnp.bfloat16)

        each_y(part, lambda copy: copy.start())
    if steps * STEP > sent:
        for part in range(parts):
            came[part, pl.ds(sent, steps * STEP - sent), :] = jnp.zeros(
                (steps * STEP - sent, PART), jnp.bfloat16
            )

    def arrived(slot):
        return t_copy(0, 0, slot, twin).wait_recv()

    def from_above(k):
        arrived(k)

        @pl.when(depth > 0)
        def _():
            down_copy(k).start()

        x_gather[k].start()
        c_gather[k].start()

    def from_below(k):
        arrived(outer - k)

        @pl.when(depth < outer - 1)
        def _():
            up_copy(k).start()

        x_gather[outer - k].start()
        c_gather[outer - k].start()

    def crossed(s):
        x_gather[s].wait_recv()
        c_gather[outer + s].start()

    def both(k, above, below):
        @pl.when(depth + k <= outer - 1)
        def _():
            above(k)

        @pl.when(depth >= k)
        def _():
            below(k)

    for k in range(1, outer):
        both(k, from_above, from_below)
        if k == 1:
            crossed(0)
        else:
            both(k - 1, crossed, lambda back: crossed(outer - back))
    squares[...] = jnp.zeros_like(squares)
    near[...] = jnp.zeros_like(near)

    def score(group):
        rows_at = pl.ds(group * quarter_k, quarter_k)

        @pl.loop(0, steps)
        def _(c):
            at = pl.ds(pl.multiple_of(c * STEP, STEP), STEP)
            block = table[rows_at, at]
            near[rows_at, :] += dot(block, xf[c], NN)
            wide = block.astype(jnp.float32)
            wide = wide * wide
            total = wide[:, :PART]
            for lane in range(PART, STEP, PART):
                total += wide[:, lane : lane + PART]
            squares[rows_at, :] += total

    score(0)
    for s in range(outer):
        c_gather[s].wait_recv()
    score(2)
    both(outer - 1, crossed, lambda back: crossed(outer - back))
    score(1)
    for s in range(outer, 2 * outer):
        c_gather[s].wait_recv()
    score(3)

    norm = jnp.sum(squares[...], axis=1, keepdims=True)
    weights[:, pl.ds(0, slots)] = column_weights(near[...], norm, width, native)

    last = width % CHUNK
    chunks = width // CHUNK + 1

    def column(c):
        return pl.multiple_of(lax.rem(c + chunks - 1, chunks) * CHUNK, CHUNK)

    def weigh(c, parts_in, native_in):
        place = column(c)
        at = pl.ds(place, CHUNK)
        within = pl.ds(pl.multiple_of(place % STEP, CHUNK), CHUNK)
        block = [xf[place // STEP, within]] if native_in else []
        block += [came[part, at, :] for part in parts_in]
        first_lane = 0 if native_in else slots + parts_in[0] * PART
        count = (slots if native_in else 0) + len(parts_in) * PART
        return dot(
            weights[:, pl.ds(first_lane, count)],
            block[0] if len(block) == 1 else jnp.concatenate(block, axis=1), NT,
        )

    def begin_sums():
        @pl.loop(0, AHEAD)
        def _(c):
            sums = weigh(c, list(range(parts - 1)), True)
            csend[c] = sums[half_k:]
            keep[c] = sums[:half_k]

    for part in range(parts):
        if part == parts - 1:
            begin_sums()
        cross[...] = jnp.zeros_like(cross)

        @pl.loop(0, steps)
        def _(c):
            @pl.when(c < whole)
            def _():
                y_copy(part, c).wait_recv()

            @pl.when(c == whole)
            def _():
                y_copy(part, whole, last_rows).wait_recv()

            at = pl.ds(pl.multiple_of(c * STEP, STEP), STEP)
            cross[...] += dot(table[:, at], came[part, at, :], NN)

        flag = came[part, pl.ds(width // 16 * 16, 16), :].astype(jnp.float32)
        flag = flag[width % 16 : width % 16 + 1]
        weights[:, pl.ds(slots + part * PART, PART)] = column_weights(
            cross[...], norm, width, flag
        )

    def narrow(c, ref, sums):
        ref[...] = sums.astype(WIRE)

        @pl.when(c == 0)
        def _():
            low = last // PART * PART
            tile = sums[:, low : low + PART]
            lost = pltpu.roll(tile - tile.astype(WIRE).astype(jnp.float32), 1, 1)
            lane = lax.broadcasted_iota(jnp.int32, tile.shape, 1)
            tile = jnp.where(lane == last - low + 1, tile + lost, tile)
            ref[:, low : low + PART] = tile.astype(WIRE)

    def c_copy(c):
        return remote(csend.at[c], crecv.at[c], c_out.at[c], c_in.at[c], (side, twin))

    def x_copy(c):
        return remote(xsend.at[c], xrecv.at[c], x_out.at[c], x_in.at[c], (side, across))

    def z_copy(c, d):
        return remote(
            zsend.at[c, d - 1], zrecv.at[c, d - 1],
            z_out.at[c, d - 1], z_in.at[c, d - 1], (side, along[d - 1]),
        )

    def add_up(c):
        @pl.when(c < AHEAD)
        def _():
            sums = weigh(c, [parts - 1], False)
            csend[c] += sums[half_k:]
            c_copy(c).start()
            keep[c] += sums[:half_k]

        @pl.when(c >= AHEAD)
        def _():
            sums = weigh(c, list(range(parts)), True)
            csend[c] = sums[half_k:]
            c_copy(c).start()
            keep[c] = sums[:half_k]

    def zt_copy(d):
        return remote(
            zturn.at[d - 1], zcame.at[d - 1], zt_out.at[d - 1], zt_in.at[d - 1],
            (side, along[d - 1]),
        )

    def xt_copy():
        return remote(xturn, xcame, xt_out.at[0], xt_in.at[0], (side, across))

    def turn_along(c):
        c_copy(c).wait_recv()
        sums = keep[c] + crecv[c]
        for d in range(1, outer):
            near_rows = sums[d * shard : (d + 1) * shard]
            far_rows = sums[quarter_k + d * shard : quarter_k + (d + 1) * shard]
            zturn[d - 1, pl.ds(0, shard), :] = near_rows.astype(WIRE)
            zturn[d - 1, pl.ds(shard, shard), :] = far_rows.astype(WIRE)
            zt_copy(d).start()
        keept[pl.ds(0, shard), :] = sums[:shard]
        keept[pl.ds(shard, shard), :] = sums[quarter_k : quarter_k + shard]

    def turn_across():
        sums = keept[...]
        for d in range(1, outer):
            zt_copy(d).wait_recv()
            sums += zcame[d - 1].astype(jnp.float32)
        xturn[...] = sums[shard:].astype(WIRE)
        xt_copy().start()
        keept[pl.ds(0, shard), :] = sums[:shard]

    def to_across(c):
        c_copy(c).wait_recv()
        sums = keep[c] + crecv[c]
        narrow(c, xsend.at[c], sums[quarter_k:])
        x_copy(c).start()
        keepx[c] = sums[:quarter_k]

    def to_along(c):
        x_copy(c).wait_recv()
        sums = keepx[c] + xrecv[c].astype(jnp.float32)
        for d in range(1, outer):
            narrow(c, zsend.at[c, d - 1], sums[d * shard : (d + 1) * shard])
        for d in range(1, outer):
            z_copy(c, d).start()
        keepx[c, pl.ds(0, shard), :] = sums[:shard]

    @pl.loop(0, chunks + 1)
    def _(c):
        @pl.when(c < chunks)
        def _():
            add_up(c)

        @pl.when((c > 0) & (c <= chunks) & (c != TURN + 1))
        def _():
            to_across(c - 1)

        @pl.when(c == TURN + 1)
        def _():
            turn_along(TURN)

        @pl.when((c >= LAG) & (c != LAG + TURN))
        def _():
            to_along(c - LAG)

    def total(c):
        sums = keepx[c, pl.ds(0, shard), :]
        for d in range(1, outer):
            z_copy(c, d).wait_recv()
            sums += zrecv[c, d - 1].astype(jnp.float32)
        return sums

    def finish(c):
        means_ref[:, pl.ds(column(c), CHUNK)] = total(c) / (mass + 1.0)
        sent_chunk(c)

    def sent_chunk(c):
        c_copy(c).wait_send()
        x_copy(c).wait_send()
        for d in range(1, outer):
            z_copy(c, d).wait_send()

    sums = total(0)
    mass = sums[:, last : last + 1] + sums[:, last + 1 : last + 2]
    means_ref[:, pl.ds(width - last, last)] = sums[:, :last] / (mass + 1.0)
    turned = jnp.sum(jnp.where(diagonal, mass, 0.0), axis=0, keepdims=True)
    occupancy_ref[...] = turned * scale
    sent_chunk(0)
    pl.loop(TURN + 1, TURN + 3)(finish)
    to_along(chunks - 3)
    turn_across()
    to_along(chunks - 2)
    pl.loop(TURN + 3, TURN + 5)(finish)
    to_along(chunks - 1)
    for copy in x_gather + c_gather:
        copy.wait_send()
    for k in range(outer - 1):
        @pl.when((depth > 0) & (depth + k <= outer - 1))
        def _():
            down_copy(k).wait_send()

        @pl.when((depth < outer - 1) & (depth >= k))
        def _():
            up_copy(k).wait_send()

    for part in range(parts):
        each_y(part, lambda copy: copy.wait_send())
    xt_copy().wait_recv()
    sums = keept[pl.ds(0, shard), :] + xcame[...].astype(jnp.float32)
    means_ref[:, pl.ds(column(TURN), CHUNK)] = sums / (mass + 1.0)
    c_copy(TURN).wait_send()
    xt_copy().wait_send()
    for d in range(1, outer):
        zt_copy(d).wait_send()
    pl.loop(TURN + 5, chunks)(finish)


def y_rows(width):
    return round_up(width + 1, 16)


def fused(frames, labels, counts, seeds):
    slots, width = frames.shape
    shard = seeds.shape[1]
    n_rows = lax.axis_size("rows")
    outer = n_rows // 4
    whole_k = shard * n_rows
    parts = slots // 2 // PART
    padded = round_up(width + 1, STEP)
    steps = padded // STEP
    chunks = width // CHUNK + 1
    total_slots = slots * lax.axis_size("half") * n_rows
    scale = 2.0 * whole_k / total_slots
    dma = pltpu.SemaphoreType.DMA
    bf16, f32 = jnp.bfloat16, jnp.float32
    flops = 4 * (slots + slots // 2) * whole_k * width
    vmem = pl.BlockSpec(memory_space=pltpu.VMEM)
    hbm = pl.BlockSpec(memory_space=pltpu.HBM)
    means, occupancy = pl.pallas_call(
        functools.partial(level, outer, width, scale),
        out_shape=(
            jax.ShapeDtypeStruct((shard, width), f32),
            jax.ShapeDtypeStruct((1, shard), f32),
        ),
        in_specs=[
            hbm,
            hbm, hbm, pl.BlockSpec(memory_space=pltpu.SMEM), hbm,
        ],
        out_specs=(vmem, vmem),
        scratch_shapes=[
            pltpu.VMEM((1, slots), jnp.int32),
            pltpu.VMEM((1, shard), jnp.int32),
            pltpu.VMEM((EIGHT, slots), bf16),
            pltpu.VMEM((steps, STEP, slots), bf16),
            pltpu.VMEM((whole_k, padded), bf16),
            pltpu.VMEM((parts, padded, PART), bf16),
            pltpu.VMEM((parts, padded, PART), bf16),
            pltpu.VMEM((whole_k, PART), f32),
            pltpu.VMEM((whole_k, PART), f32),
            pltpu.VMEM((whole_k, slots), f32),
            pltpu.VMEM((whole_k, slots + parts * PART), bf16),
            pltpu.VMEM((chunks, whole_k // 2, CHUNK), f32),
            pltpu.VMEM((chunks, whole_k // 2, CHUNK), f32),
            pltpu.VMEM((chunks, whole_k // 2, CHUNK), f32),
            pltpu.VMEM((chunks, whole_k // 4, CHUNK), f32),
            pltpu.VMEM((chunks, whole_k // 4, CHUNK), WIRE),
            pltpu.VMEM((chunks, whole_k // 4, CHUNK), WIRE),
            pltpu.VMEM((chunks, outer - 1, shard, CHUNK), WIRE),
            pltpu.VMEM((chunks, outer - 1, shard, CHUNK), WIRE),
            pltpu.VMEM((2 * shard, CHUNK), f32),
            pltpu.VMEM((outer - 1, 2 * shard, CHUNK), WIRE),
            pltpu.VMEM((outer - 1, 2 * shard, CHUNK), WIRE),
            pltpu.VMEM((shard, CHUNK), WIRE),
            pltpu.VMEM((shard, CHUNK), WIRE),
            dma((3,)), dma((steps,)), dma((parts, steps)), dma((parts, steps)),
            dma((outer,)), dma((outer,)),
            dma((4 * outer,)), dma((4 * outer,)),
            dma((chunks,)), dma((chunks,)),
            dma((chunks,)), dma((chunks,)),
            dma((chunks, outer - 1)), dma((chunks, outer - 1)),
            dma((outer - 1,)), dma((outer - 1,)), dma((1,)), dma((1,)),
        ],
        compiler_params=pltpu.CompilerParams(
            collective_id=0, has_side_effects=True, vmem_limit_bytes=52 * 2**20
        ),
        cost_estimate=pl.CostEstimate(
            flops=flops, bytes_accessed=slots * width * 2, transcendentals=slots * whole_k
        ),
    )(
        frames.T, frames.T.reshape(width // EIGHT, EIGHT, slots),
        pltpu.with_memory_space_constraint(labels[None], pltpu.HBM), counts,
        pltpu.with_memory_space_constraint(seeds, pltpu.HBM),
    )
    return (means[None], occupancy)


def fits(mesh, frames, seeds):
    sizes = dict(mesh.shape)
    n_half, n_rows = sizes["half"], sizes["rows"]
    slots = frames.shape[0] // (n_half * n_rows)
    shard = seeds.shape[1] // n_rows
    lone = frames.shape[1] % EIGHT == 0 and frames.shape[1] % STEP > 0 and frames.shape[1] % PART < PART - 1
    return (
        n_half == 2 and n_rows % 4 == 0 and n_rows >= 8 and shard % 16 == 0 and shard > 0
        and slots % (2 * PART) == 0 and slots * n_half * n_rows == frames.shape[0]
        and slots <= 1024 and seeds.shape[1] <= 512 and frames.shape[1] <= 4096
        and frames.shape[1] // CHUNK >= max(BACK, TURN + 6) and lone
    )


def solution(mesh):
    placed = (
        P(("half", "rows"), None),
        P(("half", "rows")),
        P(("half", "rows")),
        P("half", "rows"),
    )

    def run(frames, labels, counts, seeds):
        body = fused if fits(mesh, frames, seeds) else shards
        return jax.shard_map(
            body,
            mesh=mesh,
            in_specs=placed,
            out_specs=(P("half", "rows", None), P("half", "rows")),
            check_vma=False,
        )(frames, labels, counts, seeds)

    return run
```

```python
import functools
import math

import jax
import jax.numpy as jnp
from jax import lax
from jax.experimental import pallas as pl
from jax.experimental.pallas import tpu as pltpu
from jax.sharding import PartitionSpec as P


def from_partner(value, axis, stride):
    mask = 2**stride
    pairs = [(source, source ^ mask) for source in range(lax.axis_size(axis))]
    return lax.ppermute(value, axis, pairs)


def score_piece(rows_in, piece):
    cross = lax.dot_general(
        rows_in, piece, (((1,), (1,)), ((), ())), preferred_element_type=jnp.float32
    )
    wide = piece.astype(jnp.float32)
    return (cross - 0.5 * jnp.sum(wide * wide, axis=1)[None, :]) / math.sqrt(rows_in.shape[1])


def soft_weights(logits, valid):
    top = jnp.max(logits, axis=1, keepdims=True)
    expo = jnp.exp(logits - top)
    total = jnp.sum(expo, axis=1, keepdims=True)
    return (expo / total * valid[:, None]).astype(jnp.bfloat16)


def weighted(weights, rows_in):
    return lax.dot_general(
        weights, rows_in, (((0,), (0,)), ((), ())), preferred_element_type=jnp.float32
    )


def column_mass(weights):
    return jnp.sum(weights.astype(jnp.float32), axis=0)


def shards(frames, labels, counts, seeds):
    rows_dev = frames.shape[0]
    cap = rows_dev // 2
    side = lax.axis_index("half")
    spots = jnp.arange(rows_dev, dtype=jnp.int32)
    live = spots < counts[0]
    foreign = live & (labels != side)
    native = (live & (labels == side)).astype(jnp.float32)
    order = jnp.argsort(jnp.where(foreign, 0, 1).astype(jnp.int32), stable=True)
    picked = order[:cap]
    moved = frames[picked]
    flag = foreign[picked].astype(jnp.float32)
    mine = frames[seeds[0]]
    got_rows, got_flag = from_partner((moved, flag.astype(jnp.bfloat16)), "half", 0)
    pool = jnp.concatenate([frames, got_rows], axis=0)
    valid = jnp.concatenate([native, got_flag.astype(jnp.float32)])
    logits = score_piece(pool, lax.all_gather(mine, "rows", axis=0, tiled=True))
    weights = soft_weights(logits, valid)
    sums, mass = (
        lax.psum_scatter(weighted(weights, pool), "rows", scatter_dimension=0, tiled=True),
        lax.psum_scatter(column_mass(weights), "rows", scatter_dimension=0, tiled=True),
    )
    whole_k = mass.shape[0] * lax.axis_size("rows")
    total_slots = rows_dev * lax.axis_size("half") * lax.axis_size("rows")
    means = sums / (mass + 1.0)[:, None]
    occupancy = mass * (2.0 * whole_k / total_slots)
    return (means[None], occupancy[None])


MESH = pl.DeviceIdType.MESH
WIRE = jnp.bfloat16
STEP = 512
TILE = 16
EIGHT = 8
CHUNK = 256
EARLY = 1
AHEAD = 3
PART = 128
LAG = 4
TURN = 1
BACK = 8
NT = (((1,), (1,)), ((), ()))
NN = (((1,), (0,)), ((), ()))


def round_up(value, unit):
    return -(-value // unit) * unit


def dot(a, b, how):
    return lax.dot_general(a, b, how, preferred_element_type=jnp.float32)


def column_weights(cross, norm, width, valid):
    logits = (cross - 0.5 * norm) / math.sqrt(width)
    top = jnp.max(logits, axis=0, keepdims=True)
    expo = jnp.exp(logits - top)
    total = jnp.sum(expo, axis=0, keepdims=True)
    return (expo / total * valid).astype(jnp.bfloat16)


def level(
    outer, width, scale,
    x_ref, odd_ref, labels_hbm, counts_ref, seeds_hbm,
    means_ref, occupancy_ref,
    labels_ref, seeds_ref, odd, xf, table, gone, came, squares, cross, near, weights,
    keep, csend, crecv, keepx, xsend, xrecv, zsend, zrecv,
    keept, zturn, zcame, xturn, xcame,
    small_load, x_load, y_out, y_in, u_out, d_out, t_out, t_in, c_out, c_in, x_out, x_in, z_out, z_in, zt_out, zt_in, xt_out, xt_in,
):
    slots = xf.shape[2]
    shard = seeds_ref.shape[1]
    steps = xf.shape[0]
    parts = gone.shape[0]
    sent = y_rows(width)
    whole = steps - 1
    rest = width - whole * STEP
    half_k = keep.shape[1]
    quarter_k = keepx.shape[1]
    side = lax.axis_index("half")
    row = lax.axis_index("rows")
    twin = row + 1 - 2 * (row % 2)
    across = row + 2 - 4 * ((row // 2) % 2)
    along = [
        ((row // 4 + d) % outer) * 4 + row % 4 for d in range(1, outer)
    ]

    even = rest // TILE * TILE

    def load(c):
        if isinstance(c, int) and c == whole:
            at = pl.ds(whole * STEP, even)
            return pltpu.make_async_copy(x_ref.at[at], xf.at[c, pl.ds(0, even)], x_load.at[c])
        at = pl.ds(pl.multiple_of(c * STEP, STEP), STEP)
        return pltpu.make_async_copy(x_ref.at[at], xf.at[c], x_load.at[c])

    labels_load = pltpu.make_async_copy(labels_hbm, labels_ref, small_load.at[0])
    seeds_load = pltpu.make_async_copy(seeds_hbm, seeds_ref, small_load.at[1])
    odd_load = pltpu.make_async_copy(odd_ref.at[width // EIGHT - 1], odd, small_load.at[2])
    barrier = pltpu.get_barrier_semaphore()
    pl.semaphore_signal(barrier, inc=1, device_id=(1 - side, row), device_id_type=MESH)
    for peer in [twin, across] + along:
        pl.semaphore_signal(barrier, inc=1, device_id=(side, peer), device_id_type=MESH)

    labels_load.start()
    load(0).start()

    def remote(src, dst, out_sem, in_sem, where):
        return pltpu.make_async_remote_copy(
            src_ref=src, dst_ref=dst, send_sem=out_sem, recv_sem=in_sem,
            device_id=where, device_id_type=MESH,
        )

    @pl.loop(1, whole)
    def _(c):
        load(c).start()

    load(whole).start()
    odd_load.start()
    seeds_load.start()
    spots = lax.broadcasted_iota(jnp.int32, (1, slots), 1)
    upper = (
        lax.broadcasted_iota(jnp.int32, (slots, slots), 0)
        <= lax.broadcasted_iota(jnp.int32, (slots, slots), 1)
    ).astype(jnp.float32).astype(jnp.bfloat16)
    live = spots < counts_ref[0]
    labels_load.wait()
    labels = labels_ref[...]
    native = (live & (labels == side)).astype(jnp.float32)
    foreign = jnp.where(live & (labels != side), 1.0, 0.0)
    rank = dot(jnp.broadcast_to(foreign, (16, slots)).astype(jnp.bfloat16), upper, NN)[:1]
    place = jnp.where(foreign > 0, rank - 1.0, -1.0).astype(jnp.int32)

    def pick(part):
        lane = lax.broadcasted_iota(jnp.int32, (PART, slots), 0) + part * PART
        return (lane == place).astype(jnp.float32).astype(jnp.bfloat16)

    def y_copy(part, c, rows=STEP):
        at = pl.ds(c * STEP, rows)
        return remote(
            gone.at[part, at], came.at[part, at],
            y_out.at[part, c], y_in.at[part, c], (1 - side, row),
        )

    last_rows = sent - whole * STEP

    def each_y(part, act):
        @pl.loop(0, whole)
        def _(c):
            act(y_copy(part, c))

        act(y_copy(part, whole, last_rows))

    first = pick(0)

    def leave(c):
        at = pl.ds(pl.multiple_of(c * STEP, STEP), STEP)
        load(c).wait()
        gone[0, at, :] = dot(xf[c], first, NT).astype(jnp.bfloat16)

    for c in range(EARLY):
        leave(c)
    pl.semaphore_wait(barrier, outer + 2)
    for c in range(EARLY):
        y_copy(0, c).start()

    @pl.loop(EARLY, whole)
    def _(c):
        leave(c)
        y_copy(0, c).start()

    load(whole).wait()
    odd_load.wait()
    ones = lax.broadcasted_iota(jnp.int32, (STEP - even, slots), 0) == rest - even
    fill = ones.astype(jnp.float32)
    if rest > even:
        fill = jnp.concatenate([odd[...].astype(jnp.float32), fill[rest - even :]], axis=0)
    xf[whole, pl.ds(even, STEP - even), :] = fill.astype(jnp.bfloat16)

    gone[0, pl.ds(whole * STEP, STEP), :] = dot(xf[whole], first, NT).astype(jnp.bfloat16)
    y_copy(0, whole, last_rows).start()

    seeds_load.wait()
    seeds = jnp.broadcast_to(seeds_ref[...], (shard, shard))
    diagonal = lax.broadcasted_iota(jnp.int32, (shard, shard), 0) == lax.broadcasted_iota(
        jnp.int32, (shard, shard), 1
    )
    seed = jnp.sum(jnp.where(diagonal, seeds, 0), axis=1, keepdims=True)
    chosen = (
        lax.broadcasted_iota(jnp.int32, (shard, slots), 1) == seed
    ).astype(jnp.float32).astype(jnp.bfloat16)

    @pl.loop(0, steps)
    def _(c):
        at = pl.ds(pl.multiple_of(c * STEP, STEP), STEP)
        lane = lax.broadcasted_iota(jnp.int32, (shard, STEP), 1) + c * STEP
        mine = dot(chosen, xf[c], NT)
        table[pl.ds(0, shard), at] = jnp.where(lane < width, mine, 0.0).astype(jnp.bfloat16)

    def t_copy(index, source, target, where):
        return remote(
            table.at[pl.ds(source * shard, shard)], table.at[pl.ds(target * shard, shard)],
            t_out.at[index], t_in.at[target], (side, where),
        )

    def up_copy(k):
        where = lax.rem(row + 4, outer * 4)
        return remote(
            table.at[pl.ds((outer - k) % outer * shard, shard)],
            table.at[pl.ds((outer - k - 1) * shard, shard)],
            u_out.at[k], t_in.at[outer - k - 1], (side, where),
        )

    def down_copy(k):
        where = lax.rem(row + (outer - 1) * 4, outer * 4)
        return remote(
            table.at[pl.ds(k * shard, shard)], table.at[pl.ds((k + 1) * shard, shard)],
            d_out.at[k], t_in.at[k + 1], (side, where),
        )

    x_gather = [t_copy(s, s, outer + s, across) for s in range(outer)]
    c_gather = [t_copy(outer + s, s, 2 * outer + s, twin) for s in range(2 * outer)]
    depth = row // 4

    @pl.when(depth > 0)
    def _():
        down_copy(0).start()

    @pl.when(depth < outer - 1)
    def _():
        up_copy(0).start()

    x_gather[0].start()
    c_gather[0].start()

    for part in range(1, parts):
        later = pick(part)

        @pl.loop(0, steps)
        def _(c):
            at = pl.ds(pl.multiple_of(c * STEP, STEP), STEP)
            gone[part, at, :] = dot(xf[c], later, NT).astype(jnp.bfloat16)

        each_y(part, lambda copy: copy.start())
    if steps * STEP > sent:
        for part in range(parts):
            came[part, pl.ds(sent, steps * STEP - sent), :] = jnp.zeros(
                (steps * STEP - sent, PART), jnp.bfloat16
            )

    def arrived(slot):
        return t_copy(0, 0, slot, twin).wait_recv()

    def from_above(k):
        arrived(k)

        @pl.when(depth > 0)
        def _():
            down_copy(k).start()

        x_gather[k].start()
        c_gather[k].start()

    def from_below(k):
        arrived(outer - k)

        @pl.when(depth < outer - 1)
        def _():
            up_copy(k).start()

        x_gather[outer - k].start()
        c_gather[outer - k].start()

    def crossed(s):
        x_gather[s].wait_recv()
        c_gather[outer + s].start()

    def both(k, above, below):
        @pl.when(depth + k <= outer - 1)
        def _():
            above(k)

        @pl.when(depth >= k)
        def _():
            below(k)

    for k in range(1, outer):
        both(k, from_above, from_below)
        if k == 1:
            crossed(0)
        else:
            both(k - 1, crossed, lambda back: crossed(outer - back))
    squares[...] = jnp.zeros_like(squares)
    near[...] = jnp.zeros_like(near)

    def score(group):
        rows_at = pl.ds(group * quarter_k, quarter_k)

        @pl.loop(0, steps)
        def _(c):
            at = pl.ds(pl.multiple_of(c * STEP, STEP), STEP)
            block = table[rows_at, at]
            near[rows_at, :] += dot(block, xf[c], NN)
            wide = block.astype(jnp.float32)
            wide = wide * wide
            total = wide[:, :PART]
            for lane in range(PART, STEP, PART):
                total += wide[:, lane : lane + PART]
            squares[rows_at, :] += total

    score(0)
    for s in range(outer):
        c_gather[s].wait_recv()
    score(2)
    both(outer - 1, crossed, lambda back: crossed(outer - back))
    score(1)
    for s in range(outer, 2 * outer):
        c_gather[s].wait_recv()
    score(3)

    norm = jnp.sum(squares[...], axis=1, keepdims=True)
    weights[:, pl.ds(0, slots)] = column_weights(near[...], norm, width, native)

    last = width % CHUNK
    chunks = width // CHUNK + 1

    def column(c):
        return pl.multiple_of(lax.rem(c + chunks - 1, chunks) * CHUNK, CHUNK)

    def weigh(c, parts_in, native_in):
        place = column(c)
        at = pl.ds(place, CHUNK)
        within = pl.ds(pl.multiple_of(place % STEP, CHUNK), CHUNK)
        block = [xf[place // STEP, within]] if native_in else []
        block += [came[part, at, :] for part in parts_in]
        first_lane = 0 if native_in else slots + parts_in[0] * PART
        count = (slots if native_in else 0) + len(parts_in) * PART
        return dot(
            weights[:, pl.ds(first_lane, count)],
            block[0] if len(block) == 1 else jnp.concatenate(block, axis=1), NT,
        )

    def begin_sums():
        @pl.loop(0, AHEAD)
        def _(c):
            sums = weigh(c, list(range(parts - 1)), True)
            csend[c] = sums[half_k:]
            keep[c] = sums[:half_k]

    for part in range(parts):
        if part == parts - 1:
            begin_sums()
        cross[...] = jnp.zeros_like(cross)

        @pl.loop(0, steps)
        def _(c):
            @pl.when(c < whole)
            def _():
                y_copy(part, c).wait_recv()

            @pl.when(c == whole)
            def _():
                y_copy(part, whole, last_rows).wait_recv()

            at = pl.ds(pl.multiple_of(c * STEP, STEP), STEP)
            cross[...] += dot(table[:, at], came[part, at, :], NN)

        flag = came[part, pl.ds(width // 16 * 16, 16), :].astype(jnp.float32)
        flag = flag[width % 16 : width % 16 + 1]
        weights[:, pl.ds(slots + part * PART, PART)] = column_weights(
            cross[...], norm, width, flag
        )

    def narrow(c, ref, sums):
        ref[...] = sums.astype(WIRE)

        @pl.when(c == 0)
        def _():
            low = last // PART * PART
            tile = sums[:, low : low + PART]
            lost = pltpu.roll(tile - tile.astype(WIRE).astype(jnp.float32), 1, 1)
            lane = lax.broadcasted_iota(jnp.int32, tile.shape, 1)
            tile = jnp.where(lane == last - low + 1, tile + lost, tile)
            ref[:, low : low + PART] = tile.astype(WIRE)

    def c_copy(c):
        return remote(csend.at[c], crecv.at[c], c_out.at[c], c_in.at[c], (side, twin))

    def x_copy(c):
        return remote(xsend.at[c], xrecv.at[c], x_out.at[c], x_in.at[c], (side, across))

    def z_copy(c, d):
        return remote(
            zsend.at[c, d - 1], zrecv.at[c, d - 1],
            z_out.at[c, d - 1], z_in.at[c, d - 1], (side, along[d - 1]),
        )

    def add_up(c):
        @pl.when(c < AHEAD)
        def _():
            sums = weigh(c, [parts - 1], False)
            csend[c] += sums[half_k:]
            c_copy(c).start()
            keep[c] += sums[:half_k]

        @pl.when(c >= AHEAD)
        def _():
            sums = weigh(c, list(range(parts)), True)
            csend[c] = sums[half_k:]
            c_copy(c).start()
            keep[c] = sums[:half_k]

    def zt_copy(d):
        return remote(
            zturn.at[d - 1], zcame.at[d - 1], zt_out.at[d - 1], zt_in.at[d - 1],
            (side, along[d - 1]),
        )

    def xt_copy():
        return remote(xturn, xcame, xt_out.at[0], xt_in.at[0], (side, across))

    def turn_along(c):
        c_copy(c).wait_recv()
        sums = keep[c] + crecv[c]
        for d in range(1, outer):
            near_rows = sums[d * shard : (d + 1) * shard]
            far_rows = sums[quarter_k + d * shard : quarter_k + (d + 1) * shard]
            zturn[d - 1, pl.ds(0, shard), :] = near_rows.astype(WIRE)
            zturn[d - 1, pl.ds(shard, shard), :] = far_rows.astype(WIRE)
            zt_copy(d).start()
        keept[pl.ds(0, shard), :] = sums[:shard]
        keept[pl.ds(shard, shard), :] = sums[quarter_k : quarter_k + shard]

    def turn_across():
        sums = keept[...]
        for d in range(1, outer):
            zt_copy(d).wait_recv()
            sums += zcame[d - 1].astype(jnp.float32)
        xturn[...] = sums[shard:].astype(WIRE)
        xt_copy().start()
        keept[pl.ds(0, shard), :] = sums[:shard]

    def to_across(c):
        c_copy(c).wait_recv()
        sums = keep[c] + crecv[c]
        narrow(c, xsend.at[c], sums[quarter_k:])
        x_copy(c).start()
        keepx[c] = sums[:quarter_k]

    def to_along(c):
        x_copy(c).wait_recv()
        sums = keepx[c] + xrecv[c].astype(jnp.float32)
        for d in range(1, outer):
            narrow(c, zsend.at[c, d - 1], sums[d * shard : (d + 1) * shard])
        for d in range(1, outer):
            z_copy(c, d).start()
        keepx[c, pl.ds(0, shard), :] = sums[:shard]

    add_up(0)

    @pl.loop(1, chunks + 1)
    def _(c):
        @pl.when(c < chunks)
        def _():
            add_up(c)

        @pl.when((c > 0) & (c <= chunks) & (c != TURN + 1))
        def _():
            to_across(c - 1)

        @pl.when(c == TURN + 1)
        def _():
            turn_along(TURN)

        @pl.when((c >= LAG) & (c != LAG + TURN))
        def _():
            to_along(c - LAG)

    def total(c):
        sums = keepx[c, pl.ds(0, shard), :]
        for d in range(1, outer):
            z_copy(c, d).wait_recv()
            sums += zrecv[c, d - 1].astype(jnp.float32)
        return sums

    def finish(c):
        means_ref[:, pl.ds(column(c), CHUNK)] = total(c) / (mass + 1.0)
        sent_chunk(c)

    def sent_chunk(c):
        c_copy(c).wait_send()
        x_copy(c).wait_send()
        for d in range(1, outer):
            z_copy(c, d).wait_send()

    sums = total(0)
    mass = sums[:, last : last + 1] + sums[:, last + 1 : last + 2]
    means_ref[:, pl.ds(width - last, last)] = sums[:, :last] / (mass + 1.0)
    turned = jnp.sum(jnp.where(diagonal, mass, 0.0), axis=0, keepdims=True)
    occupancy_ref[...] = turned * scale
    sent_chunk(0)
    pl.loop(TURN + 1, TURN + 3)(finish)
    to_along(chunks - 3)
    turn_across()
    to_along(chunks - 2)
    pl.loop(TURN + 3, TURN + 5)(finish)
    to_along(chunks - 1)
    for copy in x_gather + c_gather:
        copy.wait_send()
    for k in range(outer - 1):
        @pl.when((depth > 0) & (depth + k <= outer - 1))
        def _():
            down_copy(k).wait_send()

        @pl.when((depth < outer - 1) & (depth >= k))
        def _():
            up_copy(k).wait_send()

    for part in range(parts):
        each_y(part, lambda copy: copy.wait_send())
    xt_copy().wait_recv()
    sums = keept[pl.ds(0, shard), :] + xcame[...].astype(jnp.float32)
    means_ref[:, pl.ds(column(TURN), CHUNK)] = sums / (mass + 1.0)
    c_copy(TURN).wait_send()
    xt_copy().wait_send()
    for d in range(1, outer):
        zt_copy(d).wait_send()
    pl.loop(TURN + 5, chunks)(finish)


def y_rows(width):
    return round_up(width + 1, 16)


def fused(frames, labels, counts, seeds):
    slots, width = frames.shape
    shard = seeds.shape[1]
    n_rows = lax.axis_size("rows")
    outer = n_rows // 4
    whole_k = shard * n_rows
    parts = slots // 2 // PART
    padded = round_up(width + 1, STEP)
    steps = padded // STEP
    chunks = width // CHUNK + 1
    total_slots = slots * lax.axis_size("half") * n_rows
    scale = 2.0 * whole_k / total_slots
    dma = pltpu.SemaphoreType.DMA
    bf16, f32 = jnp.bfloat16, jnp.float32
    flops = 4 * (slots + slots // 2) * whole_k * width
    vmem = pl.BlockSpec(memory_space=pltpu.VMEM)
    hbm = pl.BlockSpec(memory_space=pltpu.HBM)
    means, occupancy = pl.pallas_call(
        functools.partial(level, outer, width, scale),
        out_shape=(
            jax.ShapeDtypeStruct((shard, width), f32),
            jax.ShapeDtypeStruct((1, shard), f32),
        ),
        in_specs=[
            hbm,
            hbm, hbm, pl.BlockSpec(memory_space=pltpu.SMEM), hbm,
        ],
        out_specs=(vmem, vmem),
        scratch_shapes=[
            pltpu.VMEM((1, slots), jnp.int32),
            pltpu.VMEM((1, shard), jnp.int32),
            pltpu.VMEM((EIGHT, slots), bf16),
            pltpu.VMEM((steps, STEP, slots), bf16),
            pltpu.VMEM((whole_k, padded), bf16),
            pltpu.VMEM((parts, padded, PART), bf16),
            pltpu.VMEM((parts, padded, PART), bf16),
            pltpu.VMEM((whole_k, PART), f32),
            pltpu.VMEM((whole_k, PART), f32),
            pltpu.VMEM((whole_k, slots), f32),
            pltpu.VMEM((whole_k, slots + parts * PART), bf16),
            pltpu.VMEM((chunks, whole_k // 2, CHUNK), f32),
            pltpu.VMEM((chunks, whole_k // 2, CHUNK), f32),
            pltpu.VMEM((chunks, whole_k // 2, CHUNK), f32),
            pltpu.VMEM((chunks, whole_k // 4, CHUNK), f32),
            pltpu.VMEM((chunks, whole_k // 4, CHUNK), WIRE),
            pltpu.VMEM((chunks, whole_k // 4, CHUNK), WIRE),
            pltpu.VMEM((chunks, outer - 1, shard, CHUNK), WIRE),
            pltpu.VMEM((chunks, outer - 1, shard, CHUNK), WIRE),
            pltpu.VMEM((2 * shard, CHUNK), f32),
            pltpu.VMEM((outer - 1, 2 * shard, CHUNK), WIRE),
            pltpu.VMEM((outer - 1, 2 * shard, CHUNK), WIRE),
            pltpu.VMEM((shard, CHUNK), WIRE),
            pltpu.VMEM((shard, CHUNK), WIRE),
            dma((3,)), dma((steps,)), dma((parts, steps)), dma((parts, steps)),
            dma((outer,)), dma((outer,)),
            dma((4 * outer,)), dma((4 * outer,)),
            dma((chunks,)), dma((chunks,)),
            dma((chunks,)), dma((chunks,)),
            dma((chunks, outer - 1)), dma((chunks, outer - 1)),
            dma((outer - 1,)), dma((outer - 1,)), dma((1,)), dma((1,)),
        ],
        compiler_params=pltpu.CompilerParams(
            collective_id=0, has_side_effects=True, vmem_limit_bytes=52 * 2**20
        ),
        cost_estimate=pl.CostEstimate(
            flops=flops, bytes_accessed=slots * width * 2, transcendentals=slots * whole_k
        ),
    )(
        frames.T, frames.T.reshape(width // EIGHT, EIGHT, slots),
        pltpu.with_memory_space_constraint(labels[None], pltpu.HBM), counts,
        pltpu.with_memory_space_constraint(seeds, pltpu.HBM),
    )
    return (means[None], occupancy)


def fits(mesh, frames, seeds):
    sizes = dict(mesh.shape)
    n_half, n_rows = sizes["half"], sizes["rows"]
    slots = frames.shape[0] // (n_half * n_rows)
    shard = seeds.shape[1] // n_rows
    lone = frames.shape[1] % EIGHT == 0 and frames.shape[1] % STEP > 0 and frames.shape[1] % PART < PART - 1
    return (
        n_half == 2 and n_rows % 4 == 0 and n_rows >= 8 and shard % 16 == 0 and shard > 0
        and slots % (2 * PART) == 0 and slots * n_half * n_rows == frames.shape[0]
        and slots <= 1024 and seeds.shape[1] <= 512 and frames.shape[1] <= 4096
        and frames.shape[1] // CHUNK >= max(BACK, TURN + 6) and lone
    )


def solution(mesh):
    placed = (
        P(("half", "rows"), None),
        P(("half", "rows")),
        P(("half", "rows")),
        P("half", "rows"),
    )

    def run(frames, labels, counts, seeds):
        body = fused if fits(mesh, frames, seeds) else shards
        return jax.shard_map(
            body,
            mesh=mesh,
            in_specs=placed,
            out_specs=(P("half", "rows", None), P("half", "rows")),
            check_vma=False,
        )(frames, labels, counts, seeds)

    return run
```
